256 devices in a mesh: space: 64 (over z, x, core), dir: 4 (over y).
Axes of the slice: x: 4, y: 4, z: 8, core: 2. Of those that a mesh axis runs over, the one named last changes fastest.
Arguments:
- directions: bfloat16 [128, 512, 2048], P('dir', 'space'), may hold values from -16 to 16
- depth_coef: float32 [512, 2048], P('space'), may hold values from 0.5 to 2
- sensitivity: float32 [512, 2048], P('space'), may hold values from 0.4 to 1.6
- obs_weight: float32 [512, 2048], P('space'), may hold values from 0.4 to 1.6
Outputs:
- basis: bfloat16 [128, 512, 2048], P('dir', 'space')
- factor: float32 [128, 128], replicated
The draws below stay inside these ranges and needn't reach their ends.
All inputs are finite; a program needn't handle non-finite values.
Results may differ from the reference program's by a relative error of at most 0.001.
Values may be sent and summed in bfloat16 or wider, within the bound.
A program may use at most 64 MiB of HBM per device.

```python
import math
import jax
import jax.numpy as jnp
from jax import lax

K = 128
NC = 2048
NR = 512
CELLS = 1048576


def draw_directions(key, part):
    common = 8
    rows = jnp.arange(NR, dtype=jnp.float32)
    ramp = 1.0 + 2.0 * rows / max(NR - 1, 1)
    first, second, third = jax.random.split(key, 3)
    weights = jnp.clip(jax.random.normal(third, (K, common), jnp.float32), -3.0, 3.0)
    own = jnp.clip(jax.random.normal(first, (K, NR, NC), jnp.float32), -4.0, 4.0)
    shared = jnp.clip(jax.random.normal(second, (common, NR, NC), jnp.float32), -4.0, 4.0)
    scale = ramp[:, None]
    mixed = own
    for index in range(common):
        mixed = mixed + weights[:, index][:, None, None] * shared[index][None]
    values = mixed / 3.0
    return jnp.clip(values * scale[None], -16.0, 16.0).astype(jnp.bfloat16)


def steps_of(key, shape, pieces, smallest, top_value):
    def one(dim, blocks):
        steps = jax.random.uniform(jax.random.fold_in(jax.random.fold_in(key, 6), dim), (blocks,), jnp.float32, smallest / len(pieces), top_value / len(pieces))
        return jnp.repeat(jnp.exp(steps), shape[dim] // blocks).reshape((-1,) + (1,) * (len(shape) - dim - 1))

    loudness = one(*pieces[0])
    for cut in pieces[1:]:
        loudness = loudness * one(*cut)
    return loudness


def setup_inputs(seed: int = 0) -> dict:
    arg_keys = jax.random.split(jax.random.key(seed), 5)
    directions = draw_directions(jax.random.fold_in(arg_keys[4], 71), 0)
    depth_coef = jnp.clip(jnp.exp(math.log(2.0) - 1.3862944 * jax.random.uniform(arg_keys[1], (NR, NC), jnp.float32) ** steps_of(arg_keys[1], (NR, NC), ((0, 64),), -0.2, 0.2)), 0.5, 2.0)
    sensitivity = jnp.clip(jnp.exp(math.log(1.6) - 1.3862944 * jax.random.uniform(arg_keys[2], (NR, NC), jnp.float32) ** steps_of(arg_keys[2], (NR, NC), ((0, 64),), -0.2, 0.2)), 0.4, 1.6)
    obs_weight = jnp.clip(jnp.exp(math.log(1.6) - 1.3862944 * jax.random.uniform(arg_keys[3], (NR, NC), jnp.float32) ** steps_of(arg_keys[3], (NR, NC), ((0, 64),), -0.2, 0.2)), 0.4, 1.6)
    return {"directions": directions, "depth_coef": depth_coef, "sensitivity": sensitivity, "obs_weight": obs_weight}


def laplace(extended):
    inner = extended[..., 1:-1, :]
    padded = jnp.pad(inner, [(0, 0)] * (inner.ndim - 1) + [(1, 1)])
    return extended[..., :-2, :] + extended[..., 2:, :] + padded[..., :-2] + padded[..., 2:] - 4.0 * inner

def pad_rows(field):
    return jnp.pad(field, ((0, 0), (1, 1), (0, 0)))

def reference(directions, depth_coef, sensitivity, obs_weight):
    group_size = math.gcd(K, 16)

    def apply_block(block):
        field = block.astype(jnp.float32)
        prior = field + 0.1 * laplace(pad_rows(field))
        state_one = sensitivity * prior
        state_two = state_one + 0.1 * depth_coef * laplace(pad_rows(state_one)) + sensitivity * prior
        misfit = obs_weight * state_two
        adjoint = misfit + 0.1 * laplace(pad_rows(depth_coef * misfit))
        source = sensitivity * (misfit + adjoint)
        return field + source + 0.1 * laplace(pad_rows(source))
    sketch = lax.map(apply_block, directions.reshape(K // group_size, group_size, NR, NC))
    sketch = sketch.reshape(K, CELLS)
    upper = jnp.linalg.qr(sketch.T, mode='r')
    signs = jnp.sign(jnp.diagonal(upper))
    factor = upper * signs[:, None] / math.sqrt(CELLS)
    basis_rows = lax.linalg.triangular_solve(factor.T, sketch, left_side=True, lower=True)
    return (basis_rows.reshape(K, NR, NC).astype(jnp.bfloat16), factor)
```

```python
import functools

import jax
import jax.numpy as jnp
from jax import lax
from jax.experimental import pallas as pl
from jax.experimental.pallas import tpu as pltpu
from jax.sharding import PartitionSpec as P

MESH = pl.DeviceIdType.MESH
F32 = jnp.float32
BF16 = jnp.bfloat16
HALO = 4


def nt_dot(a, b):
    return lax.dot_general(a, b, (((1,), (1,)), ((), ())), preferred_element_type=F32)


def nn_dot(a, b):
    return lax.dot_general(a, b, (((1,), (0,)), ((), ())), preferred_element_type=F32)


def split(x):
    high = x.astype(BF16)
    return high, (x - high.astype(F32)).astype(BF16)


def factor_and_inverse(gram):
    size = gram.shape[0]
    tiles = size // 8
    eye = (lax.broadcasted_iota(jnp.int32, (size, size), 0) == lax.broadcasted_iota(jnp.int32, (size, size), 1)).astype(F32)
    left = [gram[8 * t : 8 * t + 8] for t in range(tiles)]
    right = [eye[8 * t : 8 * t + 8] for t in range(tiles)]
    sub = lax.broadcasted_iota(jnp.int32, (8, 1), 0)
    for k in range(size):
        p, i = divmod(k, 8)
        scale = lax.rsqrt(left[p][i : i + 1, k : k + 1])
        row_left = left[p][i : i + 1] * scale
        row_right = right[p][i : i + 1] * scale
        for t in range(p, tiles):
            col = left[t][:, k : k + 1] * scale
            if t == p:
                here = sub == i
                col = jnp.where(sub > i, col, 0.0)
                left[t] = jnp.where(here, row_left, left[t] - col * row_left)
                right[t] = jnp.where(here, row_right, right[t] - col * row_right)
            else:
                left[t] = left[t] - col * row_left
                right[t] = right[t] - col * row_right
    upper = jnp.concatenate(left, axis=0)
    keep = lax.broadcasted_iota(jnp.int32, (size, size), 0) <= lax.broadcasted_iota(jnp.int32, (size, size), 1)
    return jnp.where(keep, upper, 0.0), jnp.concatenate(right, axis=0)


def sketch_kernel(
    cfg, dirs_ref, depth_ref, sens_ref, obs_ref, out_ref, factor_ref,
    turned, packs, main, halos, coef, coef_own, coef_in, both, gram, part, part_b, part_c, result,
    y_send, y_recv, s_send, s_recv, c_send, c_recv, g_send, g_recv, o_send, o_recv, own_sem,
):
    nd, ns, nx, nz, rows, cols, dirs, total_cells = cfg
    quarter = cols // nd
    wide = quarter + 128
    group = dirs // nd
    ext = rows + 2 * HALO
    na, nb = nx * nd, nz * 2
    tile = dirs // na

    s = lax.axis_index("space")
    d = lax.axis_index("dir")
    z, x, c = s // (2 * nx), (s // 2) % nx, s % 2
    ia = x * nd + d
    ib = z * 2 + c
    down, up = lax.rem(s + ns - 1, ns), lax.rem(s + 1, ns)

    def at_a(k):
        i = lax.rem(ia + k, na)
        return i, {"space": (z * nx + i // nd) * 2 + c, "dir": lax.rem(i, nd)}

    def at_b(k):
        i = lax.rem(ib + k, nb)
        return {"space": ((i // 2) * nx + x) * 2 + lax.rem(i, 2), "dir": d}

    barrier = pltpu.get_barrier_semaphore()
    peers = [{"space": s, "dir": lax.rem(d + k, nd)} for k in range(1, nd)]
    peers += [{"space": down, "dir": d}, {"space": up, "dir": d}]
    peers += [at_a(k)[1] for k in range(1, na)] + [at_b(k) for k in range(1, nb)]
    for peer in peers:
        pl.semaphore_signal(barrier, inc=1, device_id=peer, device_id_type=MESH)

    lane = lax.broadcasted_iota(jnp.int32, (1, 128), 1)
    edge = (lane < HALO) | (lane >= 128 - HALO)

    chunk = 256

    def turn(j, carry):
        here = pl.ds(pl.multiple_of(j * chunk, chunk), chunk)
        turned[:, :, here] = jnp.swapaxes(dirs_ref[:, :, here].astype(F32), 0, 1).astype(BF16)
        return carry

    lax.fori_loop(0, cols // chunk, turn, 0)

    for q in range(nd):
        packed = jnp.zeros((group, 128), F32)
        for r in range(rows):
            after = turned[r, :, (q + 1) * quarter : (q + 1) * quarter + 128].astype(F32) if q < nd - 1 else jnp.zeros((group, 128), F32)
            before = turned[r, :, q * quarter - 128 : q * quarter].astype(F32) if q > 0 else jnp.zeros((group, 128), F32)
            beside = jnp.where(lane < 64, after, before)
            packed = jnp.where((lane >= 8 * r) & (lane < 8 * r + 8), pltpu.roll(beside, 8 * r + HALO, 1), packed)
        packs[q] = packed.astype(BF16)

    inner = pl.ds(pl.multiple_of(d * quarter, 128), quarter)
    after = pl.ds(pl.multiple_of(jnp.minimum((d + 1) * quarter, cols - 128), 128), 128)
    before = pl.ds(pl.multiple_of(jnp.maximum(d * quarter - 128, 0), 128), 128)
    valid = ((lane < HALO) & (d < nd - 1)) | ((lane >= 128 - HALO) & (d > 0))

    def quarter_of(ref):
        return jnp.concatenate([ref[:, inner], jnp.where(lane < 64, ref[:, after], ref[:, before])], axis=1)

    inside = jnp.concatenate([jnp.ones((1, quarter), jnp.bool_), valid], axis=1)
    depth = quarter_of(depth_ref)
    coef_own[0] = jnp.where(inside, 0.1 * quarter_of(sens_ref), 0.0)
    coef_own[1] = jnp.where(inside, 20.0 / depth - 4.0, 0.0)
    coef_own[2] = jnp.where(inside, 0.1 * depth * depth * quarter_of(obs_ref), 0.0)

    pl.semaphore_wait(barrier, len(peers))

    coef_copies = []
    for side, peer in enumerate((up, down)):
        copy = pltpu.make_async_remote_copy(
            src_ref=coef_own, dst_ref=coef_in.at[side], send_sem=c_send.at[side], recv_sem=c_recv.at[side],
            device_id={"space": peer, "dir": d}, device_id_type=MESH)
        copy.start()
        coef_copies.append(copy)

    def dirs_at(g):
        return pl.ds(pl.multiple_of(g * group, group), group)

    def cols_at(q):
        return pl.ds(pl.multiple_of(q * quarter, 128), quarter)

    own_main = pltpu.make_async_copy(turned.at[:, :, cols_at(d)], main.at[pl.ds(HALO, rows), dirs_at(d), :], own_sem.at[0])
    own_pack = pltpu.make_async_copy(packs.at[d], halos.at[1, dirs_at(d), :], own_sem.at[1])
    own_main.start()
    own_pack.start()

    y_copies = {}
    for k in [1, nd - 1] + list(range(2, nd - 1)):
        if k in y_copies:
            continue
        q = lax.rem(d + k, nd)
        peer = {"space": s, "dir": q}
        copies = (
            pltpu.make_async_remote_copy(
                src_ref=turned.at[:, :, cols_at(q)], dst_ref=main.at[pl.ds(HALO, rows), dirs_at(d), :],
                send_sem=y_send.at[0, k], recv_sem=y_recv.at[0, k], device_id=peer, device_id_type=MESH),
            pltpu.make_async_remote_copy(
                src_ref=packs.at[q], dst_ref=halos.at[1, dirs_at(d), :],
                send_sem=y_send.at[1, k], recv_sem=y_recv.at[1, k], device_id=peer, device_id_type=MESH),
        )
        for copy in copies:
            copy.start()
        y_copies[k] = copies

    own_main.wait()
    own_pack.wait()

    def send_rows(k):
        g = lax.rem(d + nd - k, nd)
        copies = []
        for side, peer in enumerate((up, down)):
            source = pl.ds(rows, HALO) if side == 0 else pl.ds(HALO, HALO)
            target = pl.ds(0, HALO) if side == 0 else pl.ds(HALO + rows, HALO)
            for sort, (src, dst) in enumerate((
                (main.at[source, dirs_at(g), :], main.at[target, dirs_at(g), :]),
                (halos.at[1, dirs_at(g), :], halos.at[2 * side, dirs_at(g), :]),
            )):
                copy = pltpu.make_async_remote_copy(
                    src_ref=src, dst_ref=dst, send_sem=s_send.at[sort, side, k], recv_sem=s_recv.at[sort, side, k],
                    device_id={"space": peer, "dir": d}, device_id_type=MESH)
                copy.start()
                copies.append(copy)
        return copies

    row_copies = {0: send_rows(0)}

    for copy in coef_copies:
        copy.wait()
    for i in range(3):
        coef[i, HALO : HALO + rows] = coef_own[i]
        coef[i, 0:HALO] = jnp.where(s > 0, coef_in[0, i, rows - HALO : rows], 0.0)
        coef[i, HALO + rows : ext] = jnp.where(s < ns - 1, coef_in[1, i, 0:HALO], 0.0)

    block = 16

    def stencil(base):
        here = pl.ds(pl.multiple_of(base, block), block)

        def raw(e):
            if e < HALO:
                side, r = 0, rows - HALO + e
            elif e < HALO + rows:
                side, r = 1, e - HALO
            else:
                side, r = 2, e - HALO - rows
            beside = pltpu.roll(halos[side, here, :].astype(F32), (128 - 8 * r - HALO) % 128, 1)
            row = jnp.concatenate([main[e, here, :].astype(F32), jnp.where(edge, beside, 0.0)], axis=1)
            if side == 0:
                row = jnp.where(s > 0, row, 0.0)
            if side == 2:
                row = jnp.where(s < ns - 1, row, 0.0)
            return row

        def around(above, row, below):
            return (above + below) + (pltpu.roll(row, 1, 1) + pltpu.roll(row, wide - 1, 1))

        field, state, flux, source = {}, {}, {}, {}
        for e in range(ext):
            field[e] = raw(e)
            j = e - 1
            if j >= 1:
                state[j] = coef[0, j : j + 1] * (around(field[j - 1], field[j], field[j + 1]) + 6.0 * field[j])
            j = e - 2
            if j >= 2:
                flux[j] = coef[2, j : j + 1] * (around(state[j - 1], state[j], state[j + 1]) + coef[1, j : j + 1] * state[j])
            j = e - 3
            if j >= 3:
                source[j] = coef[0, j : j + 1] * (around(flux[j - 1], flux[j], flux[j + 1]) + coef[1, j : j + 1] * flux[j])
            j = e - 4
            if j >= 4:
                value = field[j] + 0.1 * (around(source[j - 1], source[j], source[j + 1]) + 6.0 * source[j])
                high, low = split(value[:, :quarter])
                both[j - HALO, here, :] = high
                both[j - HALO, pl.ds(pl.multiple_of(dirs + base, block), block), :] = low

    def stencil_group(k):
        g = lax.rem(d + nd - k, nd)

        def step(j, carry):
            stencil(g * group + j * block)
            return carry

        lax.fori_loop(0, group // block, step, 0)

    def wait_y(k):
        for copy in y_copies[k]:
            copy.wait_recv()

    def wait_rows(k):
        for copy in row_copies[k]:
            copy.wait_recv()

    order = list(y_copies)
    wait_rows(0)
    stencil_group(0)
    wait_y(order[0])
    row_copies[order[0]] = send_rows(order[0])
    for n, k in enumerate(order):
        if n + 1 < len(order):
            wait_y(order[n + 1])
            row_copies[order[n + 1]] = send_rows(order[n + 1])
        wait_rows(k)
        stencil_group(k)

    gram[...] = jnp.zeros_like(gram)

    def gram_step(r, carry):
        gram[...] += nt_dot(both[r], both[r])
        return carry

    lax.fori_loop(0, rows, gram_step, 0)
    mixed = gram[0:dirs, dirs : 2 * dirs] + gram[dirs : 2 * dirs, 0:dirs]
    local = (gram[0:dirs, 0:dirs] + gram[dirs : 2 * dirs, dirs : 2 * dirs] + mixed) * (1.0 / total_cells)
    result[...] = local.reshape(na, tile, dirs)

    def all_of(ref, count, sem):
        return pltpu.make_async_copy(ref.at[pl.ds(0, count)], ref.at[pl.ds(0, count)], sem)

    for k in range(1, na):
        i, peer = at_a(k)
        pltpu.make_async_remote_copy(
            src_ref=result.at[i], dst_ref=part.at[ia], send_sem=g_send.at[0], recv_sem=g_recv.at[0],
            device_id=peer, device_id_type=MESH).start()
    part[ia] = result[ia]
    all_of(part, na - 1, g_recv.at[0]).wait()
    part_b[ib] = jnp.sum(part[...], axis=0)
    for k in range(1, nb):
        pltpu.make_async_remote_copy(
            src_ref=part_b.at[ib], dst_ref=part_b.at[ib], send_sem=g_send.at[1], recv_sem=g_recv.at[1],
            device_id=at_b(k), device_id_type=MESH).start()
    all_of(part_b, nb - 1, g_recv.at[1]).wait()
    part_c[ia] = jnp.sum(part_b[...], axis=0)
    for k in range(1, na):
        pltpu.make_async_remote_copy(
            src_ref=part_c.at[ia], dst_ref=part_c.at[ia], send_sem=g_send.at[2], recv_sem=g_recv.at[2],
            device_id=at_a(k)[1], device_id_type=MESH).start()
    all_of(part_c, na - 1, g_recv.at[2]).wait()

    upper, inverse = factor_and_inverse(part_c[...].reshape(dirs, dirs))
    factor_ref[...] = upper
    inverse_high, inverse_low = split(inverse)
    inverse_twice = jnp.concatenate([inverse_high, inverse_high], axis=1)

    step_rows = 2

    def basis_step(j, carry):
        for t in range(step_rows):
            r = j * step_rows + t
            value = nn_dot(inverse_twice, both[r]) + nn_dot(inverse_low, both[r, 0:dirs, :])
            turned_out[r] = value.astype(BF16)
        for k in range(1, nd):
            q = lax.rem(d + k, nd)
            here = pl.ds(j * step_rows, step_rows)
            pltpu.make_async_remote_copy(
                src_ref=turned_out.at[here, dirs_at(q), :], dst_ref=out_ref.at[here, :, cols_at(d)],
                send_sem=o_send.at[0], recv_sem=o_recv.at[0],
                device_id={"space": s, "dir": q}, device_id_type=MESH).start()
        return carry

    turned_out = main.at[pl.ds(0, rows)]
    for copies in row_copies.values():
        for copy in copies:
            copy.wait_send()
    lax.fori_loop(0, rows // step_rows, basis_step, 0)
    out_ref[:, :, cols_at(d)] = turned_out[:, dirs_at(d), :]
    away = pl.ds(0, (nd - 1) * quarter)
    pltpu.make_async_copy(out_ref.at[:, :, away], out_ref.at[:, :, away], o_recv.at[0]).wait()

    for copies in y_copies.values():
        for copy in copies:
            copy.wait_send()
    all_of(part, na - 1, g_send.at[0]).wait()
    all_of(part_b, nb - 1, g_send.at[1]).wait()
    all_of(part_c, na - 1, g_send.at[2]).wait()
    pltpu.make_async_copy(out_ref.at[:, :, away], out_ref.at[:, :, away], o_send.at[0]).wait()


def order_kernel(in_ref, factor_in, out_ref, factor_out):
    chunk = 256

    def turn(j, carry):
        here = pl.ds(pl.multiple_of(j * chunk, chunk), chunk)
        out_ref[:, :, here] = jnp.swapaxes(in_ref[:, :, here].astype(F32), 0, 1).astype(BF16)
        return carry

    lax.fori_loop(0, in_ref.shape[2] // chunk, turn, 0)
    factor_out[...] = factor_in[...]


def per_device(ns, nd, directions, depth_coef, sensitivity, obs_weight):
    group, rows, cols = directions.shape
    dirs = group * nd
    nx = 4 if ns >= 8 else ns // 2
    nz = ns // (2 * nx)
    na, nb = nx * nd, nz * 2
    tile = dirs // na
    quarter = cols // nd
    wide = quarter + 128
    ext = rows + 2 * HALO
    cfg = (nd, ns, nx, nz, rows, cols, dirs, rows * ns * cols)
    vmem = pl.BlockSpec(memory_space=pltpu.VMEM)
    dma = pltpu.SemaphoreType.DMA
    turned, factor = pl.pallas_call(
        functools.partial(sketch_kernel, cfg),
        out_shape=(jax.ShapeDtypeStruct((rows, group, cols), BF16), jax.ShapeDtypeStruct((dirs, dirs), F32)),
        in_specs=[vmem] * 4,
        out_specs=(vmem, vmem),
        scratch_shapes=[
            pltpu.VMEM((rows, group, cols), BF16),
            pltpu.VMEM((nd, group, 128), BF16),
            pltpu.VMEM((ext, dirs, quarter), BF16),
            pltpu.VMEM((3, dirs, 128), BF16),
            pltpu.VMEM((3, ext, wide), F32),
            pltpu.VMEM((3, rows, wide), F32),
            pltpu.VMEM((2, 3, rows, wide), F32),
            pltpu.VMEM((rows, 2 * dirs, quarter), BF16),
            pltpu.VMEM((2 * dirs, 2 * dirs), F32),
            pltpu.VMEM((na, tile, dirs), F32),
            pltpu.VMEM((nb, tile, dirs), F32),
            pltpu.VMEM((na, tile, dirs), F32),
            pltpu.VMEM((na, tile, dirs), F32),
            dma((2, nd)), dma((2, nd)), dma((2, 2, nd)), dma((2, 2, nd)), dma((2,)), dma((2,)),
            dma((3,)), dma((3,)), dma((1,)), dma((1,)), dma((2,)),
        ],
        compiler_params=pltpu.CompilerParams(collective_id=0, has_side_effects=True, vmem_limit_bytes=40 * 2**20),
    )(directions, depth_coef, sensitivity, obs_weight)
    return pl.pallas_call(
        order_kernel,
        out_shape=(jax.ShapeDtypeStruct((group, rows, cols), BF16), jax.ShapeDtypeStruct((dirs, dirs), F32)),
        in_specs=[vmem] * 2,
        out_specs=(vmem, vmem),
        compiler_params=pltpu.CompilerParams(vmem_limit_bytes=40 * 2**20),
    )(turned, factor)


def solution(mesh):
    return jax.shard_map(
        functools.partial(per_device, mesh.shape["space"], mesh.shape["dir"]),
        mesh=mesh,
        in_specs=(P("dir", "space", None), P("space", None), P("space", None), P("space", None)),
        out_specs=(P("dir", "space", None), P()),
        check_vma=False,
    )
```

```python
import functools

import jax
import jax.numpy as jnp
from jax import lax
from jax.experimental import pallas as pl
from jax.experimental.pallas import tpu as pltpu
from jax.sharding import PartitionSpec as P

MESH = pl.DeviceIdType.MESH
F32 = jnp.float32
BF16 = jnp.bfloat16
HALO = 4


def nt_dot(a, b):
    return lax.dot_general(a, b, (((1,), (1,)), ((), ())), preferred_element_type=F32)


def nn_dot(a, b):
    return lax.dot_general(a, b, (((1,), (0,)), ((), ())), preferred_element_type=F32)


def split(x):
    high = x.astype(BF16)
    return high, (x - high.astype(F32)).astype(BF16)


def tree_sum(terms):
    terms = list(terms)
    while len(terms) > 1:
        terms = [terms[i] + terms[i + 1] if i + 1 < len(terms) else terms[i] for i in range(0, len(terms), 2)]
    return terms[0]


def factor_and_inverse(tiles):
    size = 8 * len(tiles)
    tiles = list(tiles)

    def spread(v):
        return jnp.broadcast_to(v, (8, size))

    lane = lax.broadcasted_iota(jnp.int32, (8, size), 1)
    sub = lax.broadcasted_iota(jnp.int32, (8, size), 0)
    upper, inverse = [], []
    for p in range(len(tiles)):
        x, o = tiles[p], 8 * p
        columns = [spread(x[:, o + j : o + j + 1]) for j in range(8)]
        e = {(i, j): spread(columns[j][i : i + 1]) for j in range(8) for i in range(j, 8)}
        r, l, w, q = [], {}, {}, {}
        for j in range(8):
            r.append(lax.rsqrt(e[j, j]))
            for i in range(j + 1, 8):
                l[i, j] = e[i, j] * r[j]
            for i in range(j + 1, 8):
                for k in range(j + 1, i + 1):
                    e[i, k] = e[i, k] - l[i, j] * l[k, j]
        for j in range(8):
            w[j, j] = r[j]
            for i in range(j + 1, 8):
                w[i, j] = -r[i] * tree_sum([l[i, k] * w[k, j] for k in range(j, i)])
        for i in range(8):
            for j in range(i, 8):
                q[i, j] = q[j, i] = tree_sum([w[k, i] * w[k, j] for k in range(j, 8)])
        panel = (lane >= o) & (lane < o + 8)
        rows = [spread(v) for v in jnp.split(jnp.where(panel, jnp.where(lane - o == sub, 1.0, 0.0), x), 8, axis=0)]
        scaled = [tree_sum([q[i, j] * rows[j] for j in range(8)]) for i in range(8)]
        for t in range(p + 1, len(tiles)):
            taken = tree_sum([spread(tiles[t][:, o + j : o + j + 1]) * scaled[j] for j in range(8)])
            tiles[t] = jnp.where(panel, 0.0, tiles[t]) - taken
        weights = []
        for j in range(8):
            column = jnp.where(sub == j, w[j, j], 0.0)
            for i in range(j + 1, 8):
                column = jnp.where(sub == i, w[i, j], column)
            weights.append(column)
        below = tree_sum([weights[j] * rows[j] for j in range(8)])
        above = tree_sum([weights[j] * spread(x[j : j + 1]) for j in range(8)])
        inverse.append(jnp.where(lane < o + 8, below, 0.0))
        upper.append(jnp.where(lane >= o + sub, above, 0.0))
    return jnp.concatenate(upper, axis=0), jnp.concatenate(inverse, axis=0)


def sketch_kernel(
    cfg, dirs_hbm, depth_hbm, sens_hbm, obs_hbm, out_ref, factor_ref,
    dirs_ref, depth_ref, sens_ref, obs_ref, turned, packs, main, halos, coef, coef_own, coef_in, both, gram, part, part_b, part_c, result,
    sends, y_recv, s_recv, pack_recv, own_recv, c_recv, g_recv, o_recv, own_sem, in_sem,
):
    nd, ns, nx, nz, rows, cols, dirs, total_cells = cfg
    quarter = cols // nd
    wide = quarter + 128
    group = dirs // nd
    ext = rows + 2 * HALO
    na, nb = nx * nd, nz * 2
    tile = dirs // na

    s = lax.axis_index("space")
    d = lax.axis_index("dir")
    z, x, c = s // (2 * nx), (s // 2) % nx, s % 2
    ia = x * nd + d
    ib = z * 2 + c
    down, up = lax.rem(s + ns - 1, ns), lax.rem(s + 1, ns)

    def far(offset, length):
        return min(offset, length - offset)

    off_a = sorted(((i, j) for i in range(nx) for j in range(nd)), key=lambda o: -far(o[0], nx) - far(o[1], nd))[:-1]
    off_b = sorted(((i, j) for i in range(nz) for j in range(2)), key=lambda o: -2 * far(o[0], nz) - o[1])[:-1]

    def at_a(offset):
        i, j = lax.rem(x + offset[0], nx), lax.rem(d + offset[1], nd)
        return i * nd + j, {"space": (z * nx + i) * 2 + c, "dir": j}

    def at_b(offset):
        return {"space": (lax.rem(z + offset[0], nz) * nx + x) * 2 + lax.rem(c + offset[1], 2), "dir": d}

    def send(source, target, number, arrival, peer):
        pltpu.make_async_remote_copy(
            src_ref=source, dst_ref=target, send_sem=sends.at[number], recv_sem=arrival,
            device_id=peer, device_id_type=MESH).start()

    def await_bytes(ref, sem):
        pltpu.make_async_copy(ref, ref, sem).wait()

    inputs = [
        pltpu.make_async_copy(source, target, in_sem.at[i])
        for i, (source, target) in enumerate(
            ((dirs_hbm, dirs_ref), (depth_hbm, depth_ref), (sens_hbm, sens_ref), (obs_hbm, obs_ref)))
    ]
    for copy in inputs:
        copy.start()

    barrier = pltpu.get_barrier_semaphore()
    peers = [{"space": s, "dir": lax.rem(d + k, nd)} for k in range(1, nd)]
    peers += [{"space": down, "dir": d}, {"space": up, "dir": d}]
    peers += [{"space": (z * nx + lax.rem(x + k, nx)) * 2 + c, "dir": d} for k in range(1, nx)]
    peers += [{"space": (lax.rem(z + k, nz) * nx + x) * 2 + c, "dir": d} for k in range(1, nz)]
    for peer in peers:
        pl.semaphore_signal(barrier, inc=1, device_id=peer, device_id_type=MESH)

    lane = lax.broadcasted_iota(jnp.int32, (1, 128), 1)
    edge = (lane < HALO) | (lane >= 128 - HALO)

    inputs[0].wait()
    chunk = 256

    def turn(j, carry):
        here = pl.ds(pl.multiple_of(j * chunk, chunk), chunk)
        turned[:, :, here] = jnp.swapaxes(dirs_ref[:, :, here].astype(F32), 0, 1).astype(BF16)
        return carry

    lax.fori_loop(0, cols // chunk, turn, 0)

    for q in range(nd):
        packed = jnp.zeros((group, 128), F32)
        for r in range(rows):
            after = turned[r, :, (q + 1) * quarter : (q + 1) * quarter + 128].astype(F32) if q < nd - 1 else jnp.zeros((group, 128), F32)
            before = turned[r, :, q * quarter - 128 : q * quarter].astype(F32) if q > 0 else jnp.zeros((group, 128), F32)
            beside = jnp.where(lane < 64, after, before)
            packed = jnp.where((lane >= 8 * r) & (lane < 8 * r + 8), pltpu.roll(beside, 8 * r + HALO, 1), packed)
        packs[q] = packed.astype(BF16)

    for copy in inputs[1:]:
        copy.wait()
    inner = pl.ds(pl.multiple_of(d * quarter, 128), quarter)
    after = pl.ds(pl.multiple_of(jnp.minimum((d + 1) * quarter, cols - 128), 128), 128)
    before = pl.ds(pl.multiple_of(jnp.maximum(d * quarter - 128, 0), 128), 128)
    valid = ((lane < HALO) & (d < nd - 1)) | ((lane >= 128 - HALO) & (d > 0))

    def quarter_of(ref):
        return jnp.concatenate([ref[:, inner], jnp.where(lane < 64, ref[:, after], ref[:, before])], axis=1)

    inside = jnp.concatenate([jnp.ones((1, quarter), jnp.bool_), valid], axis=1)
    depth = quarter_of(depth_ref)
    coef_own[0] = jnp.where(inside, 0.1 * quarter_of(sens_ref), 0.0)
    coef_own[1] = jnp.where(inside, 20.0 / depth - 4.0, 0.0)
    coef_own[2] = jnp.where(inside, 0.1 * depth * depth * quarter_of(obs_ref), 0.0)

    pl.semaphore_wait(barrier, len(peers))

    above, below = {"space": up, "dir": d}, {"space": down, "dir": d}
    block = 16
    halves = group // block
    parts = 2
    part_cols = quarter // parts

    def dirs_at(g):
        return pl.ds(pl.multiple_of(g * group, group), group)

    def cols_at(q):
        return pl.ds(pl.multiple_of(q * quarter, 128), quarter)

    def place(h, k, count=1):
        return pl.ds((h * nd + k) * block, count * block)

    own_copies = [pltpu.make_async_copy(packs.at[d], halos.at[1, 0], own_sem.at[0])]
    for h in range(halves):
        own_copies.append(pltpu.make_async_copy(
            turned.at[:, pl.ds(h * block, block), cols_at(d)], main.at[pl.ds(HALO, rows), place(h, 0), :], own_sem.at[1 + h]))
    for copy in own_copies:
        copy.start()
    for k in range(1, nd):
        q = lax.rem(d + k, nd)
        send(packs.at[q], halos.at[1, k], 0, pack_recv.at[0], {"space": s, "dir": q})
    for side, peer in enumerate((above, below)):
        send(coef_own, coef_in.at[side], 1, c_recv.at[0], peer)
    for h in range(halves):
        here = pl.ds(h * block, block)
        send(turned.at[pl.ds(rows - HALO, HALO), here, cols_at(d)], main.at[pl.ds(0, HALO), place(h, 0), :], 2, own_recv.at[0], above)
        send(turned.at[pl.ds(0, HALO), here, cols_at(d)], main.at[pl.ds(HALO + rows, HALO), place(h, 0), :], 2, own_recv.at[0], below)
    for h in range(halves):
        for p in range(parts):
            for k in list(range(2, nd)) + [1]:
                q = lax.rem(d + k, nd)
                there = pl.ds(pl.multiple_of(q * quarter + p * part_cols, 128), part_cols)
                send(turned.at[:, pl.ds(h * block, block), there],
                     main.at[pl.ds(HALO, rows), place(h, k), pl.ds(p * part_cols, part_cols)],
                     3, y_recv.at[h * parts + p], {"space": s, "dir": q})
    for copy in own_copies:
        copy.wait()

    await_bytes(coef_in, c_recv.at[0])
    for i in range(3):
        coef[i, HALO : HALO + rows] = coef_own[i]
        coef[i, 0:HALO] = jnp.where(s > 0, coef_in[0, i, rows - HALO : rows], 0.0)
        coef[i, HALO + rows : ext] = jnp.where(s < ns - 1, coef_in[1, i, 0:HALO], 0.0)

    await_bytes(halos.at[1, pl.ds(0, nd - 1)], pack_recv.at[0])
    for side, peer in enumerate((above, below)):
        send(halos.at[1], halos.at[2 * side], 4, pack_recv.at[1], peer)

    def forward(h, p):
        await_bytes(main.at[pl.ds(0, rows), pl.ds(0, (nd - 1) * block), pl.ds(0, part_cols)], y_recv.at[h * parts + p])
        here = place(h, 1, nd - 1)
        there = pl.ds(p * part_cols, part_cols)
        send(main.at[pl.ds(rows, HALO), here, there], main.at[pl.ds(0, HALO), here, there], 5, s_recv.at[h * parts + p], above)
        send(main.at[pl.ds(HALO, HALO), here, there], main.at[pl.ds(HALO + rows, HALO), here, there], 5, s_recv.at[h * parts + p], below)

    def await_rows(h, p):
        await_bytes(main.at[pl.ds(0, 2 * HALO), pl.ds(0, (nd - 1) * block), pl.ds(0, part_cols)], s_recv.at[h * parts + p])


    def stencil(h, k):
        held = pl.ds(pl.multiple_of((h * nd + k) * block, block), block)
        base = lax.rem(d + nd - k, nd) * group + h * block
        here = pl.ds(pl.multiple_of(base, block), block)

        def raw(e):
            if e < HALO:
                side, r = 0, rows - HALO + e
            elif e < HALO + rows:
                side, r = 1, e - HALO
            else:
                side, r = 2, e - HALO - rows
            beside = pltpu.roll(halos[side, k, h * block : (h + 1) * block, :].astype(F32), (128 - 8 * r - HALO) % 128, 1)
            row = jnp.concatenate([main[e, held, :].astype(F32), jnp.where(edge, beside, 0.0)], axis=1)
            if side == 0:
                row = jnp.where(s > 0, row, 0.0)
            if side == 2:
                row = jnp.where(s < ns - 1, row, 0.0)
            return row

        def around(above, row, below):
            return (above + below) + (pltpu.roll(row, 1, 1) + pltpu.roll(row, wide - 1, 1))

        field, state, flux, source = {}, {}, {}, {}
        for e in range(ext):
            field[e] = raw(e)
            j = e - 1
            if j >= 1:
                state[j] = coef[0, j : j + 1] * (around(field[j - 1], field[j], field[j + 1]) + 6.0 * field[j])
            j = e - 2
            if j >= 2:
                flux[j] = coef[2, j : j + 1] * (around(state[j - 1], state[j], state[j + 1]) + coef[1, j : j + 1] * state[j])
            j = e - 3
            if j >= 3:
                source[j] = coef[0, j : j + 1] * (around(flux[j - 1], flux[j], flux[j + 1]) + coef[1, j : j + 1] * flux[j])
            j = e - 4
            if j >= 4:
                value = field[j] + 0.1 * (around(source[j - 1], source[j], source[j + 1]) + 6.0 * source[j])
                high, low = split(value[:, :quarter])
                both[j - HALO, here, :] = high
                both[j - HALO, pl.ds(pl.multiple_of(dirs + base, block), block), :] = low

    def stencils(h, first, last):
        def step(k, carry):
            stencil(h, k)
            return carry

        lax.fori_loop(first, last, step, 0)

    stages = [(h, p) for h in range(halves) for p in range(parts)]
    forward(*stages[0])
    await_bytes(main.at[pl.ds(0, 2 * HALO), pl.ds(0, halves * block), :], own_recv.at[0])
    await_bytes(halos.at[pl.ds(0, 2)], pack_recv.at[1])
    stencils(0, 0, 1)
    forward(*stages[1])
    stencils(1, 0, 1)
    forward(*stages[2])
    for p in range(parts):
        await_rows(0, p)
    stencils(0, 1, 2)
    forward(*stages[3])
    stencils(0, 2, nd)
    for p in range(parts):
        await_rows(1, p)
    stencils(1, 1, nd)

    gram[...] = jnp.zeros_like(gram)

    def gram_step(r, carry):
        gram[...] += nt_dot(both[r], both[r])
        return carry

    lax.fori_loop(0, rows, gram_step, 0)
    mixed = gram[0:dirs, dirs : 2 * dirs] + gram[dirs : 2 * dirs, 0:dirs]
    local = (gram[0:dirs, 0:dirs] + gram[dirs : 2 * dirs, dirs : 2 * dirs] + mixed) * (1.0 / total_cells)
    result[...] = local.reshape(na, tile, dirs)

    for offset in off_a:
        i, peer = at_a(offset)
        send(result.at[i], part.at[ia], 6, g_recv.at[0], peer)
    part[ia] = result[ia]
    await_bytes(part.at[pl.ds(0, na - 1)], g_recv.at[0])
    part_b[ib] = jnp.sum(part[...], axis=0)
    for offset in off_b:
        send(part_b.at[ib], part_b.at[ib], 7, g_recv.at[1], at_b(offset))
    await_bytes(part_b.at[pl.ds(0, nb - 1)], g_recv.at[1])
    part_c[ia] = jnp.sum(part_b[...], axis=0)
    for offset in off_a:
        send(part_c.at[ia], part_c.at[ia], 8, g_recv.at[2], at_a(offset)[1])
    await_bytes(part_c.at[pl.ds(0, na - 1)], g_recv.at[2])

    whole = part_c[...].reshape(dirs, dirs)
    upper, inverse = factor_and_inverse([whole[t : t + 8] for t in range(0, dirs, 8)])
    factor_ref[...] = upper
    inverse_high, inverse_low = split(inverse)
    inverse_twice = jnp.concatenate([inverse_high, inverse_high], axis=1)

    step_rows = 2
    turned_out = main.at[pl.ds(0, rows)]
    await_bytes(main.at[:, pl.ds(0, (nd - 1) * block), :], sends.at[5])

    def basis_step(j, carry):
        for t in range(step_rows):
            r = j * step_rows + t
            value = nn_dot(inverse_twice, both[r]) + nn_dot(inverse_low, both[r, 0:dirs, :])
            turned_out[r] = value.astype(BF16)
        for k in list(range(2, nd)) + [1]:
            q = lax.rem(d + k, nd)
            here = pl.ds(j * step_rows, step_rows)
            send(turned_out.at[here, dirs_at(q), :], out_ref.at[here, :, cols_at(d)], 9, o_recv.at[0], {"space": s, "dir": q})
        return carry

    lax.fori_loop(0, rows // step_rows, basis_step, 0)
    own_out = pltpu.make_async_copy(turned_out.at[:, dirs_at(d), :], out_ref.at[:, :, cols_at(d)], own_sem.at[1])
    own_out.start()
    await_bytes(halos.at[1, pl.ds(0, nd - 1)], sends.at[0])
    await_bytes(coef_in, sends.at[1])
    await_bytes(main.at[pl.ds(0, 2 * HALO), pl.ds(0, halves * block), :], sends.at[2])
    await_bytes(turned.at[:, :, pl.ds(0, (nd - 1) * quarter)], sends.at[3])
    await_bytes(halos.at[pl.ds(0, 2)], sends.at[4])
    await_bytes(part.at[pl.ds(0, na - 1)], sends.at[6])
    await_bytes(part_b.at[pl.ds(0, nb - 1)], sends.at[7])
    await_bytes(part_c.at[pl.ds(0, na - 1)], sends.at[8])
    own_out.wait()
    away = pl.ds(0, (nd - 1) * quarter)
    await_bytes(out_ref.at[:, :, away], o_recv.at[0])
    await_bytes(out_ref.at[:, :, away], sends.at[9])


def order_kernel(in_ref, factor_in, out_hbm, factor_out, ordered, out_sem, factor_sem):
    count = out_sem.shape[0]
    chunk = in_ref.shape[2] // count
    factor_copy = pltpu.make_async_copy(factor_in, factor_out, factor_sem.at[0])
    factor_copy.start()
    out = []
    for i in range(count):
        here = slice(i * chunk, (i + 1) * chunk)
        ordered[:, :, here] = jnp.swapaxes(in_ref[:, :, here].astype(F32), 0, 1).astype(BF16)
        there = pl.ds(i * chunk, chunk)
        out.append(pltpu.make_async_copy(ordered.at[:, :, there], out_hbm.at[:, :, there], out_sem.at[i]))
        out[i].start()
    for i in range(count):
        out[i].wait()
    factor_copy.wait()


def per_device(ns, nd, directions, depth_coef, sensitivity, obs_weight):
    group, rows, cols = directions.shape
    dirs = group * nd
    nx = 4 if ns >= 8 else ns // 2
    nz = ns // (2 * nx)
    na, nb = nx * nd, nz * 2
    tile = dirs // na
    quarter = cols // nd
    wide = quarter + 128
    ext = rows + 2 * HALO
    cfg = (nd, ns, nx, nz, rows, cols, dirs, rows * ns * cols)
    dma = pltpu.SemaphoreType.DMA
    turned, factor = pl.pallas_call(
        functools.partial(sketch_kernel, cfg),
        out_shape=(jax.ShapeDtypeStruct((rows, group, cols), BF16), jax.ShapeDtypeStruct((dirs, dirs), F32)),
        in_specs=[pl.BlockSpec(memory_space=pltpu.HBM)] * 4,
        out_specs=(pl.BlockSpec(memory_space=pltpu.VMEM),) * 2,
        scratch_shapes=[
            pltpu.VMEM((group, rows, cols), BF16),
            pltpu.VMEM((rows, cols), F32),
            pltpu.VMEM((rows, cols), F32),
            pltpu.VMEM((rows, cols), F32),
            pltpu.VMEM((rows, group, cols), BF16),
            pltpu.VMEM((nd, group, 128), BF16),
            pltpu.VMEM((ext, dirs, quarter), BF16),
            pltpu.VMEM((3, nd, group, 128), BF16),
            pltpu.VMEM((3, ext, wide), F32),
            pltpu.VMEM((3, rows, wide), F32),
            pltpu.VMEM((2, 3, rows, wide), F32),
            pltpu.VMEM((rows, 2 * dirs, quarter), BF16),
            pltpu.VMEM((2 * dirs, 2 * dirs), F32),
            pltpu.VMEM((na, tile, dirs), F32),
            pltpu.VMEM((nb, tile, dirs), F32),
            pltpu.VMEM((na, tile, dirs), F32),
            pltpu.VMEM((na, tile, dirs), F32),
            dma((10,)), dma((4,)), dma((4,)), dma((2,)), dma((1,)), dma((1,)), dma((3,)), dma((1,)), dma((3,)), dma((4,)),
        ],
        compiler_params=pltpu.CompilerParams(collective_id=0, has_side_effects=True, vmem_limit_bytes=40 * 2**20),
    )(*(pltpu.with_memory_space_constraint(x, pltpu.HBM) for x in (directions, depth_coef, sensitivity, obs_weight)))
    return pl.pallas_call(
        order_kernel,
        out_shape=(jax.ShapeDtypeStruct((group, rows, cols), BF16), jax.ShapeDtypeStruct((dirs, dirs), F32)),
        in_specs=[pl.BlockSpec(memory_space=pltpu.VMEM)] * 2,
        out_specs=(pl.BlockSpec(memory_space=pltpu.HBM),) * 2,
        scratch_shapes=[pltpu.VMEM((group, rows, cols), BF16), dma((4,)), dma((1,))],
        compiler_params=pltpu.CompilerParams(vmem_limit_bytes=40 * 2**20),
    )(turned, factor)


def solution(mesh):
    return jax.shard_map(
        functools.partial(per_device, mesh.shape["space"], mesh.shape["dir"]),
        mesh=mesh,
        in_specs=(P("dir", "space", None), P("space", None), P("space", None), P("space", None)),
        out_specs=(P("dir", "space", None), P()),
        check_vma=False,
    )
```

```python
import functools

import jax
import jax.numpy as jnp
from jax import lax
from jax.experimental import pallas as pl
from jax.experimental.pallas import tpu as pltpu
from jax.sharding import PartitionSpec as P

MESH = pl.DeviceIdType.MESH
F32 = jnp.float32
BF16 = jnp.bfloat16
HALO = 4


def nt_dot(a, b):
    return lax.dot_general(a, b, (((1,), (1,)), ((), ())), preferred_element_type=F32)


def nn_dot(a, b):
    return lax.dot_general(a, b, (((1,), (0,)), ((), ())), preferred_element_type=F32)


def split(x):
    high = x.astype(BF16)
    return high, (x - high.astype(F32)).astype(BF16)


def tree_sum(terms):
    terms = list(terms)
    while len(terms) > 1:
        terms = [terms[i] + terms[i + 1] if i + 1 < len(terms) else terms[i] for i in range(0, len(terms), 2)]
    return terms[0]


def factor_and_inverse(tiles):
    size = 8 * len(tiles)
    tiles = list(tiles)

    def spread(v):
        return jnp.broadcast_to(v, (8, size))

    lane = lax.broadcasted_iota(jnp.int32, (8, size), 1)
    sub = lax.broadcasted_iota(jnp.int32, (8, size), 0)
    upper, inverse = [], []
    for p in range(len(tiles)):
        x, o = tiles[p], 8 * p
        columns = [spread(x[:, o + j : o + j + 1]) for j in range(8)]
        e = {(i, j): spread(columns[j][i : i + 1]) for j in range(8) for i in range(j, 8)}
        r, l, w, q = [], {}, {}, {}
        for j in range(8):
            r.append(lax.rsqrt(e[j, j]))
            for i in range(j + 1, 8):
                l[i, j] = e[i, j] * r[j]
            for i in range(j + 1, 8):
                for k in range(j + 1, i + 1):
                    e[i, k] = e[i, k] - l[i, j] * l[k, j]
        for j in range(8):
            w[j, j] = r[j]
            for i in range(j + 1, 8):
                w[i, j] = -r[i] * tree_sum([l[i, k] * w[k, j] for k in range(j, i)])
        for i in range(8):
            for j in range(i, 8):
                q[i, j] = q[j, i] = tree_sum([w[k, i] * w[k, j] for k in range(j, 8)])
        panel = (lane >= o) & (lane < o + 8)
        rows = [spread(v) for v in jnp.split(jnp.where(panel, jnp.where(lane - o == sub, 1.0, 0.0), x), 8, axis=0)]
        scaled = [tree_sum([q[i, j] * rows[j] for j in range(8)]) for i in range(8)]
        for t in range(p + 1, len(tiles)):
            taken = tree_sum([spread(tiles[t][:, o + j : o + j + 1]) * scaled[j] for j in range(8)])
            tiles[t] = jnp.where(panel, 0.0, tiles[t]) - taken
        weights = []
        for j in range(8):
            column = jnp.where(sub == j, w[j, j], 0.0)
            for i in range(j + 1, 8):
                column = jnp.where(sub == i, w[i, j], column)
            weights.append(column)
        below = tree_sum([weights[j] * rows[j] for j in range(8)])
        above = tree_sum([weights[j] * spread(x[j : j + 1]) for j in range(8)])
        inverse.append(jnp.where(lane < o + 8, below, 0.0))
        upper.append(jnp.where(lane >= o + sub, above, 0.0))
    return jnp.concatenate(upper, axis=0), jnp.concatenate(inverse, axis=0)


def sketch_kernel(
    cfg, dirs_hbm, depth_hbm, sens_hbm, obs_hbm, out_ref, factor_ref,
    dirs_ref, depth_ref, sens_ref, obs_ref, turned, packs, main, halos, coef, coef_own, coef_in, both, deal, gram, part, part_b, part_c, result,
    sends, y_recv, s_recv, pack_recv, own_recv, c_recv, g_recv, o_recv, own_sem, in_sem,
):
    nd, ns, nx, nz, rows, cols, dirs, total_cells = cfg
    quarter = cols // nd
    wide = quarter + 128
    group = dirs // nd
    ext = rows + 2 * HALO
    na, nb = nx * nd, nz * 2
    tile = dirs // na

    s = lax.axis_index("space")
    d = lax.axis_index("dir")
    z, x, c = s // (2 * nx), (s // 2) % nx, s % 2
    ia = x * nd + d
    ib = z * 2 + c
    down, up = lax.rem(s + ns - 1, ns), lax.rem(s + 1, ns)

    def far(offset, length):
        return min(offset, length - offset)

    off_a = sorted(((i, j) for i in range(nx) for j in range(nd)), key=lambda o: -far(o[0], nx) - far(o[1], nd))[:-1]
    off_b = sorted(((i, j) for i in range(nz) for j in range(2)), key=lambda o: -2 * far(o[0], nz) - o[1])[:-1]

    def at_a(offset):
        i, j = lax.rem(x + offset[0], nx), lax.rem(d + offset[1], nd)
        return i * nd + j, {"space": (z * nx + i) * 2 + c, "dir": j}

    def at_b(offset):
        return {"space": (lax.rem(z + offset[0], nz) * nx + x) * 2 + lax.rem(c + offset[1], 2), "dir": d}

    def send(source, target, number, arrival, peer):
        pltpu.make_async_remote_copy(
            src_ref=source, dst_ref=target, send_sem=sends.at[number], recv_sem=arrival,
            device_id=peer, device_id_type=MESH).start()

    def await_bytes(ref, sem):
        pltpu.make_async_copy(ref, ref, sem).wait()

    inputs = [
        pltpu.make_async_copy(source, target, in_sem.at[i])
        for i, (source, target) in enumerate(
            ((dirs_hbm, dirs_ref), (depth_hbm, depth_ref), (sens_hbm, sens_ref), (obs_hbm, obs_ref)))
    ]
    for copy in inputs:
        copy.start()

    barrier = pltpu.get_barrier_semaphore()
    peers = [{"space": s, "dir": lax.rem(d + k, nd)} for k in range(1, nd)]
    peers += [{"space": down, "dir": d}, {"space": up, "dir": d}]
    peers += [{"space": (z * nx + lax.rem(x + k, nx)) * 2 + c, "dir": d} for k in range(1, nx)]
    peers += [{"space": (lax.rem(z + k, nz) * nx + x) * 2 + c, "dir": d} for k in range(1, nz)]
    for peer in peers:
        pl.semaphore_signal(barrier, inc=1, device_id=peer, device_id_type=MESH)

    lane = lax.broadcasted_iota(jnp.int32, (1, 128), 1)
    edge = (lane < HALO) | (lane >= 128 - HALO)

    tiles = quarter // 128
    line = lax.broadcasted_iota(jnp.int32, (quarter, quarter), 0)
    spot = lax.broadcasted_iota(jnp.int32, (quarter, quarter), 1)
    deal[...] = (lax.rem(spot, 128) * tiles + spot // 128 == line).astype(F32).astype(BF16)

    inputs[0].wait()

    def turn(q, carry):
        here = pl.ds(pl.multiple_of(q * quarter, quarter), quarter)
        dealt = nn_dot(dirs_ref[:, :, here].astype(F32).reshape(group * rows, quarter).astype(BF16), deal[...])
        turned[:, :, here] = jnp.swapaxes(dealt.reshape(group, rows, quarter), 0, 1).astype(BF16)
        return carry

    lax.fori_loop(0, nd, turn, 0)

    for q in range(nd):
        def by_row(start, there):
            return jnp.swapaxes(dirs_ref[:, :, start : start + 128].astype(F32), 0, 1) if there else jnp.zeros((rows, group, 128), F32)

        beside = jnp.where(lane < 64, by_row((q + 1) * quarter, q < nd - 1), by_row(q * quarter - 128, q > 0))
        packed = jnp.zeros((group, 128), F32)
        for r in range(rows):
            packed = jnp.where((lane >= 8 * r) & (lane < 8 * r + 8), pltpu.roll(beside[r], 8 * r + HALO, 1), packed)
        packs[q] = packed.astype(BF16)

    for copy in inputs[1:]:
        copy.wait()
    inner = pl.ds(pl.multiple_of(d * quarter, 128), quarter)
    after = pl.ds(pl.multiple_of(jnp.minimum((d + 1) * quarter, cols - 128), 128), 128)
    before = pl.ds(pl.multiple_of(jnp.maximum(d * quarter - 128, 0), 128), 128)
    valid = ((lane < HALO) & (d < nd - 1)) | ((lane >= 128 - HALO) & (d > 0))

    def quarter_of(ref):
        return jnp.concatenate([ref[:, inner], jnp.where(lane < 64, ref[:, after], ref[:, before])], axis=1)

    inside = jnp.concatenate([jnp.ones((1, quarter), jnp.bool_), valid], axis=1)
    depth = quarter_of(depth_ref)
    coef_own[0] = jnp.where(inside, 0.1 * quarter_of(sens_ref), 0.0)
    coef_own[1] = jnp.where(inside, 20.0 / depth - 4.0, 0.0)
    coef_own[2] = jnp.where(inside, 0.1 * depth * depth * quarter_of(obs_ref), 0.0)

    pl.semaphore_wait(barrier, len(peers))

    above, below = {"space": up, "dir": d}, {"space": down, "dir": d}
    block = 16
    halves = group // block

    def dirs_at(g):
        return pl.ds(pl.multiple_of(g * group, group), group)

    def cols_at(q):
        return pl.ds(pl.multiple_of(q * quarter, 128), quarter)

    blocks = [(0, h) for h in range(halves)] + [(k, h) for h in range(halves) for k in range(1, nd)]
    stages = [[halves + h * (nd - 1) + k for k in range(nd - 1)] for h in range(halves)]
    parts = 2
    width = quarter // parts

    def place(b, count=1):
        return pl.ds(b * block, count * block)

    own_copies = [pltpu.make_async_copy(packs.at[d], halos.at[1, 0], own_sem.at[0])]
    for h in range(halves):
        own_copies.append(pltpu.make_async_copy(
            turned.at[:, pl.ds(h * block, block), cols_at(d)], main.at[pl.ds(HALO, rows), place(h), :], own_sem.at[1 + h]))
    for copy in own_copies:
        copy.start()
    for k in range(1, nd):
        q = lax.rem(d + k, nd)
        send(packs.at[q], halos.at[1, k], 0, pack_recv.at[0], {"space": s, "dir": q})
    for side, peer in enumerate((above, below)):
        send(coef_own, coef_in.at[side], 1, c_recv.at[0], peer)
    for h in range(halves):
        here = pl.ds(h * block, block)
        send(turned.at[pl.ds(rows - HALO, HALO), here, cols_at(d)], main.at[pl.ds(0, HALO), place(h), :], 2, own_recv.at[0], above)
        send(turned.at[pl.ds(0, HALO), here, cols_at(d)], main.at[pl.ds(HALO + rows, HALO), place(h), :], 2, own_recv.at[0], below)
    for n, stage in enumerate(stages):
        for p in range(parts):
            for b in stage[1:] + stage[:1]:
                k, h = blocks[b]
                q = lax.rem(d + k, nd)
                there = pl.ds(pl.multiple_of(q * quarter + p * width, 128), width)
                send(turned.at[:, pl.ds(h * block, block), there],
                     main.at[pl.ds(HALO, rows), place(b), pl.ds(p * width, width)],
                     3, y_recv.at[n * parts + p], {"space": s, "dir": q})
    for copy in own_copies:
        copy.wait()

    await_bytes(coef_in, c_recv.at[0])
    for i in range(3):
        coef[i, HALO : HALO + rows] = coef_own[i]
        coef[i, 0:HALO] = jnp.where(s > 0, coef_in[0, i, rows - HALO : rows], 0.0)
        coef[i, HALO + rows : ext] = jnp.where(s < ns - 1, coef_in[1, i, 0:HALO], 0.0)
        plain = coef[i, :, 0:quarter]
        high = plain.astype(BF16)
        middle, low = split(plain - high.astype(F32))
        dealt = nn_dot(jnp.concatenate([high, middle, low], axis=0), deal[...])
        coef[i, :, 0:quarter] = (dealt[0:ext] + dealt[ext : 2 * ext]) + dealt[2 * ext : 3 * ext]

    await_bytes(halos.at[1, pl.ds(0, nd - 1)], pack_recv.at[0])
    for side, peer in enumerate((above, below)):
        send(halos.at[1], halos.at[2 * side], 4, pack_recv.at[1], peer)

    def forward(n, p):
        here, there = place(stages[n][0], len(stages[n])), pl.ds(p * width, width)
        number = n * parts + p
        await_bytes(main.at[pl.ds(0, rows), here, there], y_recv.at[number])
        send(main.at[pl.ds(rows, HALO), here, there], main.at[pl.ds(0, HALO), here, there], 5, s_recv.at[number], above)
        send(main.at[pl.ds(HALO, HALO), here, there], main.at[pl.ds(HALO + rows, HALO), here, there], 5, s_recv.at[number], below)

    def await_rows(n, p):
        here, there = place(stages[n][0], len(stages[n])), pl.ds(p * width, width)
        await_bytes(main.at[pl.ds(0, 2 * HALO), here, there], s_recv.at[n * parts + p])

    def stencil(b):
        held = pl.ds(pl.multiple_of(b * block, block), block)
        late = jnp.maximum(b - halves, 0)
        k = jnp.where(b < halves, 0, 1 + lax.rem(late, nd - 1))
        h = jnp.where(b < halves, b, late // (nd - 1))
        of_owner = pl.ds(pl.multiple_of(h * block, block), block)
        base = lax.rem(d + nd - k, nd) * group + h * block
        here = pl.ds(pl.multiple_of(base, block), block)

        first, last = lane == 0, lane == 127

        def cut(row):
            return [row[:, 128 * t : 128 * t + 128] for t in range(tiles)]

        def raw(e):
            if e < HALO:
                side, r = 0, rows - HALO + e
            elif e < HALO + rows:
                side, r = 1, e - HALO
            else:
                side, r = 2, e - HALO - rows
            beside = pltpu.roll(halos[side, k, of_owner, :].astype(F32), (128 - 8 * r - HALO) % 128, 1)
            row = cut(main[e, held, :].astype(F32)) + [jnp.where(edge, beside, 0.0)]
            if side == 0:
                row = [jnp.where(s > 0, v, 0.0) for v in row]
            if side == 2:
                row = [jnp.where(s < ns - 1, v, 0.0) for v in row]
            return row

        def beside_of(row):
            next_first, next_out = pltpu.roll(row[0], 127, 1), pltpu.roll(row[tiles], 127, 1)
            last_last, last_out = pltpu.roll(row[tiles - 1], 1, 1), pltpu.roll(row[tiles], 1, 1)
            right = row[1:tiles] + [jnp.where(last, next_out, next_first), jnp.where(last, next_first, next_out)]
            left = [jnp.where(first, last_out, last_last)] + row[0 : tiles - 1] + [jnp.where(first, last_last, last_out)]
            return [a + b for a, b in zip(left, right)]

        def of_row(n, j):
            row = coef[n, j : j + 1]
            return cut(row) + [row[:, quarter:wide]]

        def around(rows_of, j, own):
            return [
                (a + b) + (n + w * v)
                for a, b, n, w, v in zip(rows_of[j - 1], rows_of[j + 1], beside_of(rows_of[j]), own, rows_of[j])]

        def times(a, b):
            return [v * w for v, w in zip(a, b)]

        six = [6.0] * (tiles + 1)
        field, state, flux, source = {}, {}, {}, {}
        for e in range(ext):
            field[e] = raw(e)
            j = e - 1
            if j >= 1:
                state[j] = times(of_row(0, j), around(field, j, six))
            j = e - 2
            if j >= 2:
                flux[j] = times(of_row(2, j), around(state, j, of_row(1, j)))
            j = e - 3
            if j >= 3:
                source[j] = times(of_row(0, j), around(flux, j, of_row(1, j)))
            j = e - 4
            if j >= 4:
                value = [v + 0.1 * w for v, w in zip(field[j], around(source, j, six))]
                high, low = split(jnp.concatenate(value[:tiles], axis=1))
                both[j - HALO, here, :] = high
                both[j - HALO, pl.ds(pl.multiple_of(dirs + base, block), block), :] = low

    await_bytes(main.at[pl.ds(0, 2 * HALO), pl.ds(0, halves * block), :], own_recv.at[0])
    await_bytes(halos.at[pl.ds(0, 2)], pack_recv.at[1])
    before = {b: [] for b in range(len(blocks))}
    for n, stage in enumerate(stages):
        for p in range(parts):
            before[n * parts + p].append(functools.partial(forward, n, p))
    for n, stage in enumerate(stages):
        for p in range(parts):
            before[stage[0]].append(functools.partial(await_rows, n, p))

    def step(b, carry):
        for at, actions in before.items():
            if actions:
                @pl.when(b == at)
                def _():
                    for action in actions:
                        action()
        stencil(b)
        return carry

    lax.fori_loop(0, len(blocks), step, 0)

    total = nt_dot(both[0], both[0])
    for r in range(1, rows):
        total = total + nt_dot(both[r], both[r])
    gram[...] = total
    mixed = gram[0:dirs, dirs : 2 * dirs] + gram[dirs : 2 * dirs, 0:dirs]
    local = (gram[0:dirs, 0:dirs] + gram[dirs : 2 * dirs, dirs : 2 * dirs] + mixed) * (1.0 / total_cells)
    result[...] = local.reshape(na, tile, dirs)

    for offset in off_a:
        i, peer = at_a(offset)
        send(result.at[i], part.at[ia], 6, g_recv.at[0], peer)
    part[ia] = result[ia]

    deal[...] = (lax.rem(line, 128) * tiles + line // 128 == spot).astype(F32).astype(BF16)

    def undeal(r, carry):
        both[r] = nn_dot(both[r], deal[...]).astype(BF16)
        return carry

    lax.fori_loop(0, rows, undeal, 0)
    await_bytes(part.at[pl.ds(0, na - 1)], g_recv.at[0])
    part_b[ib] = jnp.sum(part[...], axis=0)
    for offset in off_b:
        send(part_b.at[ib], part_b.at[ib], 7, g_recv.at[1], at_b(offset))
    await_bytes(part_b.at[pl.ds(0, nb - 1)], g_recv.at[1])
    part_c[ia] = jnp.sum(part_b[...], axis=0)
    for offset in off_a:
        send(part_c.at[ia], part_c.at[ia], 8, g_recv.at[2], at_a(offset)[1])
    await_bytes(part_c.at[pl.ds(0, na - 1)], g_recv.at[2])

    whole = part_c[...].reshape(dirs, dirs)
    upper, inverse = factor_and_inverse([whole[t : t + 8] for t in range(0, dirs, 8)])
    factor_ref[...] = upper
    inverse_high, inverse_low = split(inverse)
    inverse_twice = jnp.concatenate([inverse_high, inverse_high], axis=1)

    step_rows = 2
    turned_out = main.at[pl.ds(0, rows)]
    await_bytes(main.at[:, pl.ds(0, (nd - 1) * block), :], sends.at[5])

    def basis_step(j, carry):
        for t in range(step_rows):
            r = j * step_rows + t
            value = nn_dot(inverse_twice, both[r]) + nn_dot(inverse_low, both[r, 0:dirs, :])
            turned_out[r] = value.astype(BF16)
        for k in list(range(2, nd)) + [1]:
            q = lax.rem(d + k, nd)
            here = pl.ds(j * step_rows, step_rows)
            send(turned_out.at[here, dirs_at(q), :], out_ref.at[here, :, cols_at(d)], 9, o_recv.at[0], {"space": s, "dir": q})
        return carry

    lax.fori_loop(0, rows // step_rows, basis_step, 0)
    own_out = pltpu.make_async_copy(turned_out.at[:, dirs_at(d), :], out_ref.at[:, :, cols_at(d)], own_sem.at[1])
    own_out.start()
    await_bytes(halos.at[1, pl.ds(0, nd - 1)], sends.at[0])
    await_bytes(coef_in, sends.at[1])
    await_bytes(main.at[pl.ds(0, 2 * HALO), pl.ds(0, halves * block), :], sends.at[2])
    await_bytes(turned.at[:, :, pl.ds(0, (nd - 1) * quarter)], sends.at[3])
    await_bytes(halos.at[pl.ds(0, 2)], sends.at[4])
    await_bytes(part.at[pl.ds(0, na - 1)], sends.at[6])
    await_bytes(part_b.at[pl.ds(0, nb - 1)], sends.at[7])
    await_bytes(part_c.at[pl.ds(0, na - 1)], sends.at[8])
    own_out.wait()
    away = pl.ds(0, (nd - 1) * quarter)
    await_bytes(out_ref.at[:, :, away], o_recv.at[0])
    await_bytes(out_ref.at[:, :, away], sends.at[9])


def order_kernel(in_ref, factor_in, out_hbm, factor_out, ordered, out_sem, factor_sem):
    count = out_sem.shape[0]
    chunk = in_ref.shape[2] // count
    factor_copy = pltpu.make_async_copy(factor_in, factor_out, factor_sem.at[0])
    factor_copy.start()
    out = []
    for i in range(count):
        here = slice(i * chunk, (i + 1) * chunk)
        ordered[:, :, here] = jnp.swapaxes(in_ref[:, :, here].astype(F32), 0, 1).astype(BF16)
        there = pl.ds(i * chunk, chunk)
        out.append(pltpu.make_async_copy(ordered.at[:, :, there], out_hbm.at[:, :, there], out_sem.at[i]))
        out[i].start()
    for i in range(count):
        out[i].wait()
    factor_copy.wait()


def per_device(ns, nd, directions, depth_coef, sensitivity, obs_weight):
    group, rows, cols = directions.shape
    dirs = group * nd
    nx = 4 if ns >= 8 else ns // 2
    nz = ns // (2 * nx)
    na, nb = nx * nd, nz * 2
    tile = dirs // na
    quarter = cols // nd
    wide = quarter + 128
    ext = rows + 2 * HALO
    cfg = (nd, ns, nx, nz, rows, cols, dirs, rows * ns * cols)
    dma = pltpu.SemaphoreType.DMA
    turned, factor = pl.pallas_call(
        functools.partial(sketch_kernel, cfg),
        out_shape=(jax.ShapeDtypeStruct((rows, group, cols), BF16), jax.ShapeDtypeStruct((dirs, dirs), F32)),
        in_specs=[pl.BlockSpec(memory_space=pltpu.HBM)] * 4,
        out_specs=(pl.BlockSpec(memory_space=pltpu.VMEM),) * 2,
        scratch_shapes=[
            pltpu.VMEM((group, rows, cols), BF16),
            pltpu.VMEM((rows, cols), F32),
            pltpu.VMEM((rows, cols), F32),
            pltpu.VMEM((rows, cols), F32),
            pltpu.VMEM((rows, group, cols), BF16),
            pltpu.VMEM((nd, group, 128), BF16),
            pltpu.VMEM((ext, dirs, quarter), BF16),
            pltpu.VMEM((3, nd, group, 128), BF16),
            pltpu.VMEM((3, ext, wide), F32),
            pltpu.VMEM((3, rows, wide), F32),
            pltpu.VMEM((2, 3, rows, wide), F32),
            pltpu.VMEM((rows, 2 * dirs, quarter), BF16),
            pltpu.VMEM((quarter, quarter), BF16),
            pltpu.VMEM((2 * dirs, 2 * dirs), F32),
            pltpu.VMEM((na, tile, dirs), F32),
            pltpu.VMEM((nb, tile, dirs), F32),
            pltpu.VMEM((na, tile, dirs), F32),
            pltpu.VMEM((na, tile, dirs), F32),
            dma((10,)), dma((4,)), dma((4,)), dma((2,)), dma((1,)), dma((1,)), dma((3,)), dma((1,)), dma((3,)), dma((4,)),
        ],
        compiler_params=pltpu.CompilerParams(collective_id=0, has_side_effects=True, vmem_limit_bytes=40 * 2**20),
    )(*(pltpu.with_memory_space_constraint(x, pltpu.HBM) for x in (directions, depth_coef, sensitivity, obs_weight)))
    return pl.pallas_call(
        order_kernel,
        out_shape=(jax.ShapeDtypeStruct((group, rows, cols), BF16), jax.ShapeDtypeStruct((dirs, dirs), F32)),
        in_specs=[pl.BlockSpec(memory_space=pltpu.VMEM)] * 2,
        out_specs=(pl.BlockSpec(memory_space=pltpu.HBM),) * 2,
        scratch_shapes=[pltpu.VMEM((group, rows, cols), BF16), dma((4,)), dma((1,))],
        compiler_params=pltpu.CompilerParams(vmem_limit_bytes=40 * 2**20),
    )(turned, factor)


def solution(mesh):
    return jax.shard_map(
        functools.partial(per_device, mesh.shape["space"], mesh.shape["dir"]),
        mesh=mesh,
        in_specs=(P("dir", "space", None), P("space", None), P("space", None), P("space", None)),
        out_specs=(P("dir", "space", None), P()),
        check_vma=False,
    )
```

```python
import functools

import jax
import jax.numpy as jnp
from jax import lax
from jax.experimental import pallas as pl
from jax.experimental.pallas import tpu as pltpu
from jax.sharding import PartitionSpec as P

MESH = pl.DeviceIdType.MESH
F32 = jnp.float32
BF16 = jnp.bfloat16
HALO = 4


def nt_dot(a, b):
    return lax.dot_general(a, b, (((1,), (1,)), ((), ())), preferred_element_type=F32)


def nn_dot(a, b):
    return lax.dot_general(a, b, (((1,), (0,)), ((), ())), preferred_element_type=F32)


def split(x):
    high = x.astype(BF16)
    return high, (x - high.astype(F32)).astype(BF16)


def tree_sum(terms):
    terms = list(terms)
    while len(terms) > 1:
        terms = [terms[i] + terms[i + 1] if i + 1 < len(terms) else terms[i] for i in range(0, len(terms), 2)]
    return terms[0]


def factor_and_inverse(tiles):
    size = 8 * len(tiles)
    tiles = list(tiles)

    def spread(v):
        return jnp.broadcast_to(v, (8, size))

    lane = lax.broadcasted_iota(jnp.int32, (8, size), 1)
    sub = lax.broadcasted_iota(jnp.int32, (8, size), 0)
    upper, inverse = [], []
    for p in range(len(tiles)):
        x, o = tiles[p], 8 * p
        columns = [spread(x[:, o + j : o + j + 1]) for j in range(8)]
        e = {(i, j): spread(columns[j][i : i + 1]) for j in range(8) for i in range(j, 8)}
        r, l, w, q = [], {}, {}, {}
        for j in range(8):
            r.append(lax.rsqrt(e[j, j]))
            for i in range(j + 1, 8):
                l[i, j] = e[i, j] * r[j]
            for i in range(j + 1, 8):
                for k in range(j + 1, i + 1):
                    e[i, k] = e[i, k] - l[i, j] * l[k, j]
        for j in range(8):
            w[j, j] = r[j]
            for i in range(j + 1, 8):
                w[i, j] = -r[i] * tree_sum([l[i, k] * w[k, j] for k in range(j, i)])
        for i in range(8):
            for j in range(i, 8):
                q[i, j] = q[j, i] = tree_sum([w[k, i] * w[k, j] for k in range(j, 8)])
        panel = (lane >= o) & (lane < o + 8)
        rows = [spread(v) for v in jnp.split(jnp.where(panel, jnp.where(lane - o == sub, 1.0, 0.0), x), 8, axis=0)]
        scaled = [tree_sum([q[i, j] * rows[j] for j in range(8)]) for i in range(8)]
        for t in range(p + 1, len(tiles)):
            taken = tree_sum([spread(tiles[t][:, o + j : o + j + 1]) * scaled[j] for j in range(8)])
            tiles[t] = jnp.where(panel, 0.0, tiles[t]) - taken
        weights = []
        for j in range(8):
            column = jnp.where(sub == j, w[j, j], 0.0)
            for i in range(j + 1, 8):
                column = jnp.where(sub == i, w[i, j], column)
            weights.append(column)
        below = tree_sum([weights[j] * rows[j] for j in range(8)])
        above = tree_sum([weights[j] * spread(x[j : j + 1]) for j in range(8)])
        inverse.append(jnp.where(lane < o + 8, below, 0.0))
        upper.append(jnp.where(lane >= o + sub, above, 0.0))
    return jnp.concatenate(upper, axis=0), jnp.concatenate(inverse, axis=0)


def sketch_kernel(
    cfg, dirs_hbm, depth_hbm, sens_hbm, obs_hbm, out_ref, factor_ref,
    dirs_ref, depth_ref, sens_ref, obs_ref, turned, packs, main, halos, coef, coef_own, coef_in, both, deal, gram, part, part_b, part_c, result,
    sends, y_recv, s_recv, pack_recv, own_recv, c_recv, g_recv, o_recv, own_sem, in_sem,
):
    nd, ns, nx, nz, rows, cols, dirs, total_cells = cfg
    quarter = cols // nd
    wide = quarter + 128
    group = dirs // nd
    ext = rows + 2 * HALO
    na, nb = nx * nd, nz * 2
    tile = dirs // na

    s = lax.axis_index("space")
    d = lax.axis_index("dir")
    z, x, c = s // (2 * nx), (s // 2) % nx, s % 2
    ia = x * nd + d
    ib = z * 2 + c
    down, up = lax.rem(s + ns - 1, ns), lax.rem(s + 1, ns)

    def far(offset, length):
        return min(offset, length - offset)

    off_a = sorted(((i, j) for i in range(nx) for j in range(nd)), key=lambda o: -far(o[0], nx) - far(o[1], nd))[:-1]
    off_b = sorted(((i, j) for i in range(nz) for j in range(2)), key=lambda o: -2 * far(o[0], nz) - o[1])[:-1]

    def at_a(offset):
        i, j = lax.rem(x + offset[0], nx), lax.rem(d + offset[1], nd)
        return i * nd + j, {"space": (z * nx + i) * 2 + c, "dir": j}

    def at_b(offset):
        return {"space": (lax.rem(z + offset[0], nz) * nx + x) * 2 + lax.rem(c + offset[1], 2), "dir": d}

    def send(source, target, number, arrival, peer):
        pltpu.make_async_remote_copy(
            src_ref=source, dst_ref=target, send_sem=sends.at[number], recv_sem=arrival,
            device_id=peer, device_id_type=MESH).start()

    def await_bytes(ref, sem):
        pltpu.make_async_copy(ref, ref, sem).wait()

    inputs = [
        pltpu.make_async_copy(source, target, in_sem.at[i])
        for i, (source, target) in enumerate(
            ((dirs_hbm, dirs_ref), (depth_hbm, depth_ref), (sens_hbm, sens_ref), (obs_hbm, obs_ref)))
    ]
    for copy in inputs:
        copy.start()

    barrier = pltpu.get_barrier_semaphore()
    peers = [{"space": s, "dir": lax.rem(d + k, nd)} for k in range(1, nd)]
    peers += [{"space": down, "dir": d}, {"space": up, "dir": d}]
    peers += [{"space": (z * nx + lax.rem(x + k, nx)) * 2 + c, "dir": d} for k in range(1, nx)]
    peers += [{"space": (lax.rem(z + k, nz) * nx + x) * 2 + c, "dir": d} for k in range(1, nz)]
    for peer in peers:
        pl.semaphore_signal(barrier, inc=1, device_id=peer, device_id_type=MESH)

    lane = lax.broadcasted_iota(jnp.int32, (1, 128), 1)
    edge = (lane < HALO) | (lane >= 128 - HALO)

    tiles = quarter // 128
    line = lax.broadcasted_iota(jnp.int32, (quarter, quarter), 0)
    spot = lax.broadcasted_iota(jnp.int32, (quarter, quarter), 1)
    deal[...] = (lax.rem(spot, 128) * tiles + spot // 128 == line).astype(F32).astype(BF16)

    inputs[0].wait()

    def turn(q, carry):
        here = pl.ds(pl.multiple_of(q * quarter, quarter), quarter)
        dealt = nn_dot(dirs_ref[:, :, here].astype(F32).reshape(group * rows, quarter).astype(BF16), deal[...])
        turned[:, :, here] = jnp.swapaxes(dealt.reshape(group, rows, quarter), 0, 1).astype(BF16)
        return carry

    lax.fori_loop(0, nd, turn, 0)

    for q in range(nd):
        def by_row(start, there):
            return jnp.swapaxes(dirs_ref[:, :, start : start + 128].astype(F32), 0, 1) if there else jnp.zeros((rows, group, 128), F32)

        beside = jnp.where(lane < 64, by_row((q + 1) * quarter, q < nd - 1), by_row(q * quarter - 128, q > 0))
        packed = jnp.zeros((group, 128), F32)
        for r in range(rows):
            packed = jnp.where((lane >= 8 * r) & (lane < 8 * r + 8), pltpu.roll(beside[r], 8 * r + HALO, 1), packed)
        packs[q] = packed.astype(BF16)

    for copy in inputs[1:]:
        copy.wait()
    inner = pl.ds(pl.multiple_of(d * quarter, 128), quarter)
    after = pl.ds(pl.multiple_of(jnp.minimum((d + 1) * quarter, cols - 128), 128), 128)
    before = pl.ds(pl.multiple_of(jnp.maximum(d * quarter - 128, 0), 128), 128)
    valid = ((lane < HALO) & (d < nd - 1)) | ((lane >= 128 - HALO) & (d > 0))

    def quarter_of(ref):
        return jnp.concatenate([ref[:, inner], jnp.where(lane < 64, ref[:, after], ref[:, before])], axis=1)

    inside = jnp.concatenate([jnp.ones((1, quarter), jnp.bool_), valid], axis=1)
    depth = quarter_of(depth_ref)
    coef_own[0] = jnp.where(inside, 0.1 * quarter_of(sens_ref), 0.0)
    coef_own[1] = jnp.where(inside, 20.0 / depth - 4.0, 0.0)
    coef_own[2] = jnp.where(inside, 0.1 * depth * depth * quarter_of(obs_ref), 0.0)

    pl.semaphore_wait(barrier, len(peers))

    above, below = {"space": up, "dir": d}, {"space": down, "dir": d}
    block = 16
    halves = group // block

    def dirs_at(g):
        return pl.ds(pl.multiple_of(g * group, group), group)

    def cols_at(q):
        return pl.ds(pl.multiple_of(q * quarter, 128), quarter)

    owners = [1, nd - 1] + list(range(2, nd - 1))
    blocks = [(0, h) for h in range(halves)] + [(k, h) for h in range(halves) for k in owners]
    final = len(blocks) - len(owners)
    stages = [list(range(b, b + len(owners))) for b in range(halves, final, len(owners))] + [[b] for b in range(final, len(blocks))]
    whole_stages = len(stages) - len(owners)
    parts = 2
    width = quarter // parts

    def place(b, count=1):
        return pl.ds(b * block, count * block)

    own_copies = [pltpu.make_async_copy(packs.at[d], halos.at[1, 0], own_sem.at[0])]
    for h in range(halves):
        own_copies.append(pltpu.make_async_copy(
            turned.at[:, pl.ds(h * block, block), cols_at(d)], main.at[pl.ds(HALO, rows), place(h), :], own_sem.at[1 + h]))
    for copy in own_copies:
        copy.start()
    for k in range(1, nd):
        q = lax.rem(d + k, nd)
        send(packs.at[q], halos.at[1, k], 0, pack_recv.at[0], {"space": s, "dir": q})
    for side, peer in enumerate((above, below)):
        send(coef_own, coef_in.at[side], 1, c_recv.at[0], peer)
    for h in range(halves):
        here = pl.ds(h * block, block)
        send(turned.at[pl.ds(rows - HALO, HALO), here, cols_at(d)], main.at[pl.ds(0, HALO), place(h), :], 2, own_recv.at[0], above)
        send(turned.at[pl.ds(0, HALO), here, cols_at(d)], main.at[pl.ds(HALO + rows, HALO), place(h), :], 2, own_recv.at[0], below)
    rounds = [[n] for n in range(whole_stages)] + [list(range(whole_stages, len(stages)))]
    for round_stages in rounds:
        for p in range(parts):
            pieces = [(n, b) for n in round_stages for b in stages[n]]
            for n, b in pieces[2:] + pieces[:2]:
                k, h = blocks[b]
                q = lax.rem(d + k, nd)
                there = pl.ds(pl.multiple_of(q * quarter + p * width, 128), width)
                send(turned.at[:, pl.ds(h * block, block), there],
                     main.at[pl.ds(HALO, rows), place(b), pl.ds(p * width, width)],
                     3, y_recv.at[n * parts + p], {"space": s, "dir": q})
    for copy in own_copies:
        copy.wait()

    await_bytes(coef_in, c_recv.at[0])
    for i in range(3):
        coef[i, HALO : HALO + rows] = coef_own[i]
        coef[i, 0:HALO] = jnp.where(s > 0, coef_in[0, i, rows - HALO : rows], 0.0)
        coef[i, HALO + rows : ext] = jnp.where(s < ns - 1, coef_in[1, i, 0:HALO], 0.0)
        plain = coef[i, :, 0:quarter]
        high = plain.astype(BF16)
        middle, low = split(plain - high.astype(F32))
        dealt = nn_dot(jnp.concatenate([high, middle, low], axis=0), deal[...])
        coef[i, :, 0:quarter] = (dealt[0:ext] + dealt[ext : 2 * ext]) + dealt[2 * ext : 3 * ext]

    await_bytes(halos.at[1, pl.ds(0, nd - 1)], pack_recv.at[0])
    for side, peer in enumerate((above, below)):
        send(halos.at[1], halos.at[2 * side], 4, pack_recv.at[1], peer)

    def forward(n, p):
        here, there = place(stages[n][0], len(stages[n])), pl.ds(p * width, width)
        number = n * parts + p
        await_bytes(main.at[pl.ds(0, rows), here, there], y_recv.at[number])
        send(main.at[pl.ds(rows, HALO), here, there], main.at[pl.ds(0, HALO), here, there], 5, s_recv.at[number], above)
        send(main.at[pl.ds(HALO, HALO), here, there], main.at[pl.ds(HALO + rows, HALO), here, there], 5, s_recv.at[number], below)

    def await_rows(n, p):
        here, there = place(stages[n][0], len(stages[n])), pl.ds(p * width, width)
        await_bytes(main.at[pl.ds(0, 2 * HALO), here, there], s_recv.at[n * parts + p])

    def stencil(b):
        held = pl.ds(pl.multiple_of(b * block, block), block)
        late = jnp.maximum(b - halves, 0)
        turn_of = lax.rem(late, nd - 1)
        k = jnp.where(b < halves, 0, jnp.where(turn_of == 0, 1, jnp.where(turn_of == 1, nd - 1, turn_of)))
        h = jnp.where(b < halves, b, late // (nd - 1))
        of_owner = pl.ds(pl.multiple_of(h * block, block), block)
        base = lax.rem(d + nd - k, nd) * group + h * block
        here = pl.ds(pl.multiple_of(base, block), block)

        first, last = lane == 0, lane == 127

        def cut(row):
            return [row[:, 128 * t : 128 * t + 128] for t in range(tiles)]

        def raw(e):
            if e < HALO:
                side, r = 0, rows - HALO + e
            elif e < HALO + rows:
                side, r = 1, e - HALO
            else:
                side, r = 2, e - HALO - rows
            beside = pltpu.roll(halos[side, k, of_owner, :].astype(F32), (128 - 8 * r - HALO) % 128, 1)
            row = cut(main[e, held, :].astype(F32)) + [jnp.where(edge, beside, 0.0)]
            if side == 0:
                row = [jnp.where(s > 0, v, 0.0) for v in row]
            if side == 2:
                row = [jnp.where(s < ns - 1, v, 0.0) for v in row]
            return row

        def beside_of(row):
            next_first, next_out = pltpu.roll(row[0], 127, 1), pltpu.roll(row[tiles], 127, 1)
            last_last, last_out = pltpu.roll(row[tiles - 1], 1, 1), pltpu.roll(row[tiles], 1, 1)
            right = row[1:tiles] + [jnp.where(last, next_out, next_first), jnp.where(last, next_first, next_out)]
            left = [jnp.where(first, last_out, last_last)] + row[0 : tiles - 1] + [jnp.where(first, last_last, last_out)]
            return [a + b for a, b in zip(left, right)]

        def of_row(n, j):
            row = coef[n, j : j + 1]
            return cut(row) + [row[:, quarter:wide]]

        def around(rows_of, j, own):
            return [
                (a + b) + (n + w * v)
                for a, b, n, w, v in zip(rows_of[j - 1], rows_of[j + 1], beside_of(rows_of[j]), own, rows_of[j])]

        def times(a, b):
            return [v * w for v, w in zip(a, b)]

        six = [6.0] * (tiles + 1)
        field, state, flux, source = {}, {}, {}, {}
        for e in range(ext):
            field[e] = raw(e)
            j = e - 1
            if j >= 1:
                state[j] = times(of_row(0, j), around(field, j, six))
            j = e - 2
            if j >= 2:
                flux[j] = times(of_row(2, j), around(state, j, of_row(1, j)))
            j = e - 3
            if j >= 3:
                source[j] = times(of_row(0, j), around(flux, j, of_row(1, j)))
            j = e - 4
            if j >= 4:
                value = [v + 0.1 * w for v, w in zip(field[j], around(source, j, six))]
                high, low = split(jnp.concatenate(value[:tiles], axis=1))
                both[j - HALO, here, :] = high
                both[j - HALO, pl.ds(pl.multiple_of(dirs + base, block), block), :] = low

    await_bytes(main.at[pl.ds(0, 2 * HALO), pl.ds(0, halves * block), :], own_recv.at[0])
    await_bytes(halos.at[pl.ds(0, 2)], pack_recv.at[1])
    before = {b: [] for b in range(len(blocks))}
    for i, round_stages in enumerate(rounds):
        for p in range(parts):
            for n in round_stages:
                before[i * parts + p].append(functools.partial(forward, n, p))
    for n, stage in enumerate(stages):
        for p in range(parts):
            before[stage[0]].append(functools.partial(await_rows, n, p))

    def step(b, carry):
        for at, actions in before.items():
            if actions:
                @pl.when(b == at)
                def _():
                    for action in actions:
                        action()
        stencil(b)
        return carry

    lax.fori_loop(0, len(blocks), step, 0)

    total = nt_dot(both[0], both[0])
    for r in range(1, rows):
        total = total + nt_dot(both[r], both[r])
    gram[...] = total
    mixed = gram[0:dirs, dirs : 2 * dirs] + gram[dirs : 2 * dirs, 0:dirs]
    local = (gram[0:dirs, 0:dirs] + gram[dirs : 2 * dirs, dirs : 2 * dirs] + mixed) * (1.0 / total_cells)
    result[...] = local.reshape(na, tile, dirs)

    for offset in off_a:
        i, peer = at_a(offset)
        send(result.at[i], part.at[ia], 6, g_recv.at[0], peer)
    part[ia] = result[ia]

    deal[...] = (lax.rem(line, 128) * tiles + line // 128 == spot).astype(F32).astype(BF16)

    def undeal(r, carry):
        both[r] = nn_dot(both[r], deal[...]).astype(BF16)
        return carry

    lax.fori_loop(0, rows, undeal, 0)
    await_bytes(part.at[pl.ds(0, na - 1)], g_recv.at[0])
    part_b[ib] = jnp.sum(part[...], axis=0)
    for offset in off_b:
        send(part_b.at[ib], part_b.at[ib], 7, g_recv.at[1], at_b(offset))
    await_bytes(part_b.at[pl.ds(0, nb - 1)], g_recv.at[1])
    part_c[ia] = jnp.sum(part_b[...], axis=0)
    for offset in off_a:
        send(part_c.at[ia], part_c.at[ia], 8, g_recv.at[2], at_a(offset)[1])
    await_bytes(part_c.at[pl.ds(0, na - 1)], g_recv.at[2])

    whole = part_c[...].reshape(dirs, dirs)
    upper, inverse = factor_and_inverse([whole[t : t + 8] for t in range(0, dirs, 8)])
    factor_ref[...] = upper
    inverse_high, inverse_low = split(inverse)
    inverse_twice = jnp.concatenate([inverse_high, inverse_high], axis=1)

    step_rows = 2
    turned_out = main.at[pl.ds(0, rows)]
    await_bytes(main.at[:, pl.ds(0, (nd - 1) * block), :], sends.at[5])

    def basis_step(j, carry):
        for t in range(step_rows):
            r = j * step_rows + t
            value = nn_dot(inverse_twice, both[r]) + nn_dot(inverse_low, both[r, 0:dirs, :])
            turned_out[r] = value.astype(BF16)
        for k in list(range(2, nd)) + [1]:
            q = lax.rem(d + k, nd)
            here = pl.ds(j * step_rows, step_rows)
            send(turned_out.at[here, dirs_at(q), :], out_ref.at[here, :, cols_at(d)], 9, o_recv.at[0], {"space": s, "dir": q})
        return carry

    lax.fori_loop(0, rows // step_rows, basis_step, 0)
    own_out = pltpu.make_async_copy(turned_out.at[:, dirs_at(d), :], out_ref.at[:, :, cols_at(d)], own_sem.at[1])
    own_out.start()
    await_bytes(halos.at[1, pl.ds(0, nd - 1)], sends.at[0])
    await_bytes(coef_in, sends.at[1])
    await_bytes(main.at[pl.ds(0, 2 * HALO), pl.ds(0, halves * block), :], sends.at[2])
    await_bytes(turned.at[:, :, pl.ds(0, (nd - 1) * quarter)], sends.at[3])
    await_bytes(halos.at[pl.ds(0, 2)], sends.at[4])
    await_bytes(part.at[pl.ds(0, na - 1)], sends.at[6])
    await_bytes(part_b.at[pl.ds(0, nb - 1)], sends.at[7])
    await_bytes(part_c.at[pl.ds(0, na - 1)], sends.at[8])
    own_out.wait()
    away = pl.ds(0, (nd - 1) * quarter)
    await_bytes(out_ref.at[:, :, away], o_recv.at[0])
    await_bytes(out_ref.at[:, :, away], sends.at[9])


def order_kernel(in_ref, factor_in, out_hbm, factor_out, ordered, out_sem, factor_sem):
    count = out_sem.shape[0]
    chunk = in_ref.shape[2] // count
    factor_copy = pltpu.make_async_copy(factor_in, factor_out, factor_sem.at[0])
    factor_copy.start()
    out = []
    for i in range(count):
        here = slice(i * chunk, (i + 1) * chunk)
        ordered[:, :, here] = jnp.swapaxes(in_ref[:, :, here].astype(F32), 0, 1).astype(BF16)
        there = pl.ds(i * chunk, chunk)
        out.append(pltpu.make_async_copy(ordered.at[:, :, there], out_hbm.at[:, :, there], out_sem.at[i]))
        out[i].start()
    for i in range(count):
        out[i].wait()
    factor_copy.wait()


def per_device(ns, nd, directions, depth_coef, sensitivity, obs_weight):
    group, rows, cols = directions.shape
    dirs = group * nd
    nx = 4 if ns >= 8 else ns // 2
    nz = ns // (2 * nx)
    na, nb = nx * nd, nz * 2
    tile = dirs // na
    quarter = cols // nd
    wide = quarter + 128
    ext = rows + 2 * HALO
    cfg = (nd, ns, nx, nz, rows, cols, dirs, rows * ns * cols)
    dma = pltpu.SemaphoreType.DMA
    turned, factor = pl.pallas_call(
        functools.partial(sketch_kernel, cfg),
        out_shape=(jax.ShapeDtypeStruct((rows, group, cols), BF16), jax.ShapeDtypeStruct((dirs, dirs), F32)),
        in_specs=[pl.BlockSpec(memory_space=pltpu.HBM)] * 4,
        out_specs=(pl.BlockSpec(memory_space=pltpu.VMEM),) * 2,
        scratch_shapes=[
            pltpu.VMEM((group, rows, cols), BF16),
            pltpu.VMEM((rows, cols), F32),
            pltpu.VMEM((rows, cols), F32),
            pltpu.VMEM((rows, cols), F32),
            pltpu.VMEM((rows, group, cols), BF16),
            pltpu.VMEM((nd, group, 128), BF16),
            pltpu.VMEM((ext, dirs, quarter), BF16),
            pltpu.VMEM((3, nd, group, 128), BF16),
            pltpu.VMEM((3, ext, wide), F32),
            pltpu.VMEM((3, rows, wide), F32),
            pltpu.VMEM((2, 3, rows, wide), F32),
            pltpu.VMEM((rows, 2 * dirs, quarter), BF16),
            pltpu.VMEM((quarter, quarter), BF16),
            pltpu.VMEM((2 * dirs, 2 * dirs), F32),
            pltpu.VMEM((na, tile, dirs), F32),
            pltpu.VMEM((nb, tile, dirs), F32),
            pltpu.VMEM((na, tile, dirs), F32),
            pltpu.VMEM((na, tile, dirs), F32),
            dma((10,)), dma((8,)), dma((8,)), dma((2,)), dma((1,)), dma((1,)), dma((3,)), dma((1,)), dma((3,)), dma((4,)),
        ],
        compiler_params=pltpu.CompilerParams(collective_id=0, has_side_effects=True, vmem_limit_bytes=40 * 2**20),
    )(*(pltpu.with_memory_space_constraint(x, pltpu.HBM) for x in (directions, depth_coef, sensitivity, obs_weight)))
    return pl.pallas_call(
        order_kernel,
        out_shape=(jax.ShapeDtypeStruct((group, rows, cols), BF16), jax.ShapeDtypeStruct((dirs, dirs), F32)),
        in_specs=[pl.BlockSpec(memory_space=pltpu.VMEM)] * 2,
        out_specs=(pl.BlockSpec(memory_space=pltpu.HBM),) * 2,
        scratch_shapes=[pltpu.VMEM((group, rows, cols), BF16), dma((4,)), dma((1,))],
        compiler_params=pltpu.CompilerParams(vmem_limit_bytes=40 * 2**20),
    )(turned, factor)


def solution(mesh):
    return jax.shard_map(
        functools.partial(per_device, mesh.shape["space"], mesh.shape["dir"]),
        mesh=mesh,
        in_specs=(P("dir", "space", None), P("space", None), P("space", None), P("space", None)),
        out_specs=(P("dir", "space", None), P()),
        check_vma=False,
    )
```

```python
import functools

import jax
import jax.numpy as jnp
from jax import lax
from jax.experimental import pallas as pl
from jax.experimental.pallas import tpu as pltpu
from jax.sharding import PartitionSpec as P

MESH = pl.DeviceIdType.MESH
F32 = jnp.float32
BF16 = jnp.bfloat16
HALO = 4


def nt_dot(a, b):
    return lax.dot_general(a, b, (((1,), (1,)), ((), ())), preferred_element_type=F32)


def nn_dot(a, b):
    return lax.dot_general(a, b, (((1,), (0,)), ((), ())), preferred_element_type=F32)


def split(x):
    high = x.astype(BF16)
    return high, (x - high.astype(F32)).astype(BF16)


def tree_sum(terms):
    terms = list(terms)
    while len(terms) > 1:
        terms = [terms[i] + terms[i + 1] if i + 1 < len(terms) else terms[i] for i in range(0, len(terms), 2)]
    return terms[0]


def factor_and_inverse(tiles):
    size = 8 * len(tiles)
    tiles = list(tiles)

    def spread(v):
        return jnp.broadcast_to(v, (8, size))

    lane = lax.broadcasted_iota(jnp.int32, (8, size), 1)
    sub = lax.broadcasted_iota(jnp.int32, (8, size), 0)
    upper, inverse = [], []
    for p in range(len(tiles)):
        x, o = tiles[p], 8 * p
        columns = [spread(x[:, o + j : o + j + 1]) for j in range(8)]
        e = {(i, j): spread(columns[j][i : i + 1]) for j in range(8) for i in range(j, 8)}
        r, l, f, unit, w = [], {}, {}, {}, {}
        for j in range(8):
            over = 1.0 / e[j, j]
            r.append(lax.rsqrt(e[j, j]))
            for i in range(j + 1, 8):
                f[i, j] = e[i, j] * over
                l[i, j] = e[i, j] * r[j]
            for i in range(j + 1, 8):
                for k in range(j + 1, i + 1):
                    e[i, k] = e[i, k] - (e[i, j] * e[k, j]) * over
        for j in range(8):
            for i in range(j + 1, 8):
                unit[i, j] = -tree_sum([f[i, j]] + [f[i, k] * unit[k, j] for k in range(j + 1, i)])
        for j in range(8):
            w[j, j] = r[j]
            for i in range(j + 1, 8):
                w[i, j] = r[i] * unit[i, j]
        panel = (lane >= o) & (lane < o + 8)
        rows = [spread(v) for v in jnp.split(jnp.where(panel, jnp.where(lane - o == sub, 1.0, 0.0), x), 8, axis=0)]
        solved = [tree_sum([w[j, i] * rows[i] for i in range(j + 1)]) for j in range(8)]
        scaled = [tree_sum([w[j, i] * solved[j] for j in range(i, 8)]) for i in range(8)]
        for t in range(p + 1, len(tiles)):
            taken = tree_sum([spread(tiles[t][:, o + j : o + j + 1]) * scaled[j] for j in range(8)])
            tiles[t] = jnp.where(panel, 0.0, tiles[t]) - taken
        below = solved[0]
        for j in range(1, 8):
            below = jnp.where(sub == j, solved[j], below)
        above = below
        for j in range(8):
            for i in range(j, 8):
                above = jnp.where((sub == j) & (lane == o + i), e[j, j] * r[j] if i == j else l[i, j], above)
        inverse.append(jnp.where(lane < o + 8, below, 0.0))
        upper.append(jnp.where(lane >= o + sub, above, 0.0))
    return jnp.concatenate(upper, axis=0), jnp.concatenate(inverse, axis=0)


def sketch_kernel(
    cfg, dirs_hbm, depth_hbm, sens_hbm, obs_hbm, out_ref, factor_ref,
    dirs_ref, depth_ref, sens_ref, obs_ref, turned, packs, main, halos, coef, coef_own, coef_in, both, values, deal, gram, part, part_b, part_c, result,
    sends, y_recv, s_recv, pack_recv, own_recv, c_recv, g_recv, o_recv, own_sem, in_sem,
):
    nd, ns, nx, nz, rows, cols, dirs, total_cells = cfg
    quarter = cols // nd
    wide = quarter + 128
    group = dirs // nd
    ext = rows + 2 * HALO
    na, nb = nx * nd, nz * 2
    tile = dirs // na

    s = lax.axis_index("space")
    d = lax.axis_index("dir")
    z, x, c = s // (2 * nx), (s // 2) % nx, s % 2
    ia = x * nd + d
    ib = z * 2 + c
    down, up = lax.rem(s + ns - 1, ns), lax.rem(s + 1, ns)

    def far(offset, length):
        return min(offset, length - offset)

    off_a = sorted(((i, j) for i in range(nx) for j in range(nd)), key=lambda o: -far(o[0], nx) - far(o[1], nd))[:-1]
    off_b = sorted(((i, j) for i in range(nz) for j in range(2)), key=lambda o: -2 * far(o[0], nz) - o[1])[:-1]

    def at_a(offset):
        i, j = lax.rem(x + offset[0], nx), lax.rem(d + offset[1], nd)
        return i * nd + j, {"space": (z * nx + i) * 2 + c, "dir": j}

    def at_b(offset):
        return {"space": (lax.rem(z + offset[0], nz) * nx + x) * 2 + lax.rem(c + offset[1], 2), "dir": d}

    def send(source, target, number, arrival, peer):
        pltpu.make_async_remote_copy(
            src_ref=source, dst_ref=target, send_sem=sends.at[number], recv_sem=arrival,
            device_id=peer, device_id_type=MESH).start()

    def await_bytes(ref, sem):
        pltpu.make_async_copy(ref, ref, sem).wait()

    inputs = [
        pltpu.make_async_copy(source, target, in_sem.at[i])
        for i, (source, target) in enumerate(
            ((dirs_hbm, dirs_ref), (depth_hbm, depth_ref), (sens_hbm, sens_ref), (obs_hbm, obs_ref)))
    ]
    for copy in inputs:
        copy.start()

    barrier = pltpu.get_barrier_semaphore()
    peers = [{"space": s, "dir": lax.rem(d + k, nd)} for k in range(1, nd)]
    peers += [{"space": down, "dir": d}, {"space": up, "dir": d}]
    peers += [{"space": (z * nx + lax.rem(x + k, nx)) * 2 + c, "dir": d} for k in range(1, nx)]
    peers += [{"space": (lax.rem(z + k, nz) * nx + x) * 2 + c, "dir": d} for k in range(1, nz)]
    for peer in peers:
        pl.semaphore_signal(barrier, inc=1, device_id=peer, device_id_type=MESH)

    lane = lax.broadcasted_iota(jnp.int32, (1, 128), 1)
    edge = (lane < HALO) | (lane >= 128 - HALO)

    tiles = quarter // 128
    line = lax.broadcasted_iota(jnp.int32, (quarter, quarter), 0)
    spot = lax.broadcasted_iota(jnp.int32, (quarter, quarter), 1)
    deal[...] = (lax.rem(spot, 128) * tiles + spot // 128 == line).astype(F32).astype(BF16)

    inputs[0].wait()

    def turn(q, carry):
        here = pl.ds(pl.multiple_of(q * quarter, quarter), quarter)
        dealt = nn_dot(dirs_ref[:, :, here].astype(F32).reshape(group * rows, quarter).astype(BF16), deal[...])
        turned[:, :, here] = jnp.swapaxes(dealt.reshape(group, rows, quarter), 0, 1).astype(BF16)
        return carry

    lax.fori_loop(0, nd, turn, 0)

    for q in range(nd):
        def by_row(start, there):
            return jnp.swapaxes(dirs_ref[:, :, start : start + 128].astype(F32), 0, 1) if there else jnp.zeros((rows, group, 128), F32)

        beside = jnp.where(lane < 64, by_row((q + 1) * quarter, q < nd - 1), by_row(q * quarter - 128, q > 0))
        packed = jnp.zeros((group, 128), F32)
        for r in range(rows):
            packed = jnp.where((lane >= 8 * r) & (lane < 8 * r + 8), pltpu.roll(beside[r], 8 * r + HALO, 1), packed)
        packs[q] = packed.astype(BF16)

    for copy in inputs[1:]:
        copy.wait()
    inner = pl.ds(pl.multiple_of(d * quarter, 128), quarter)
    after = pl.ds(pl.multiple_of(jnp.minimum((d + 1) * quarter, cols - 128), 128), 128)
    before = pl.ds(pl.multiple_of(jnp.maximum(d * quarter - 128, 0), 128), 128)
    valid = ((lane < HALO) & (d < nd - 1)) | ((lane >= 128 - HALO) & (d > 0))

    def quarter_of(ref):
        return jnp.concatenate([ref[:, inner], jnp.where(lane < 64, ref[:, after], ref[:, before])], axis=1)

    inside = jnp.concatenate([jnp.ones((1, quarter), jnp.bool_), valid], axis=1)
    depth = quarter_of(depth_ref)
    coef_own[0] = jnp.where(inside, 0.1 * quarter_of(sens_ref), 0.0)
    coef_own[1] = jnp.where(inside, 20.0 / depth - 4.0, 0.0)
    coef_own[2] = jnp.where(inside, 0.1 * depth * depth * quarter_of(obs_ref), 0.0)

    pl.semaphore_wait(barrier, len(peers))

    above, below = {"space": up, "dir": d}, {"space": down, "dir": d}
    block = 16
    halves = group // block

    def dirs_at(g):
        return pl.ds(pl.multiple_of(g * group, group), group)

    def cols_at(q):
        return pl.ds(pl.multiple_of(q * quarter, 128), quarter)

    owners = [1, nd - 1] + list(range(2, nd - 1))
    blocks = [(0, h) for h in range(halves)] + [(k, h) for h in range(halves) for k in owners]
    final = len(blocks) - len(owners)
    stages = [list(range(b, b + len(owners))) for b in range(halves, final, len(owners))] + [[b] for b in range(final, len(blocks))]
    whole_stages = len(stages) - len(owners)
    parts = 2
    width = quarter // parts

    def place(b, count=1):
        return pl.ds(b * block, count * block)

    own_copies = [pltpu.make_async_copy(packs.at[d], halos.at[1, 0], own_sem.at[0])]
    for h in range(halves):
        own_copies.append(pltpu.make_async_copy(
            turned.at[:, pl.ds(h * block, block), cols_at(d)], main.at[pl.ds(HALO, rows), place(h), :], own_sem.at[1 + h]))
    for copy in own_copies:
        copy.start()
    for k in range(1, nd):
        q = lax.rem(d + k, nd)
        send(packs.at[q], halos.at[1, k], 0, pack_recv.at[0], {"space": s, "dir": q})
    for side, peer in enumerate((above, below)):
        send(coef_own, coef_in.at[side], 1, c_recv.at[0], peer)
    for h in range(halves):
        here = pl.ds(h * block, block)
        send(turned.at[pl.ds(rows - HALO, HALO), here, cols_at(d)], main.at[pl.ds(0, HALO), place(h), :], 2, own_recv.at[0], above)
        send(turned.at[pl.ds(0, HALO), here, cols_at(d)], main.at[pl.ds(HALO + rows, HALO), place(h), :], 2, own_recv.at[0], below)
    rounds = [[n] for n in range(whole_stages)] + [list(range(whole_stages, len(stages)))]
    for round_stages in rounds:
        for p in range(parts):
            pieces = [(n, b) for n in round_stages for b in stages[n]]
            for n, b in pieces[2:] + pieces[:2]:
                k, h = blocks[b]
                q = lax.rem(d + k, nd)
                there = pl.ds(pl.multiple_of(q * quarter + p * width, 128), width)
                send(turned.at[:, pl.ds(h * block, block), there],
                     main.at[pl.ds(HALO, rows), place(b), pl.ds(p * width, width)],
                     3, y_recv.at[n * parts + p], {"space": s, "dir": q})
    for copy in own_copies:
        copy.wait()

    await_bytes(coef_in, c_recv.at[0])
    for i in range(3):
        coef[i, HALO : HALO + rows] = coef_own[i]
        coef[i, 0:HALO] = jnp.where(s > 0, coef_in[0, i, rows - HALO : rows], 0.0)
        coef[i, HALO + rows : ext] = jnp.where(s < ns - 1, coef_in[1, i, 0:HALO], 0.0)
        plain = coef[i, :, 0:quarter]
        high = plain.astype(BF16)
        middle, low = split(plain - high.astype(F32))
        dealt = nn_dot(jnp.concatenate([high, middle, low], axis=0), deal[...])
        coef[i, :, 0:quarter] = (dealt[0:ext] + dealt[ext : 2 * ext]) + dealt[2 * ext : 3 * ext]

    await_bytes(halos.at[1, pl.ds(0, nd - 1)], pack_recv.at[0])
    for side, peer in enumerate((above, below)):
        send(halos.at[1], halos.at[2 * side], 4, pack_recv.at[1], peer)

    def forward(n, p):
        here, there = place(stages[n][0], len(stages[n])), pl.ds(p * width, width)
        number = n * parts + p
        await_bytes(main.at[pl.ds(0, rows), here, there], y_recv.at[number])
        send(main.at[pl.ds(rows, HALO), here, there], main.at[pl.ds(0, HALO), here, there], 5, s_recv.at[number], above)
        send(main.at[pl.ds(HALO, HALO), here, there], main.at[pl.ds(HALO + rows, HALO), here, there], 5, s_recv.at[number], below)

    def await_rows(n, p):
        here, there = place(stages[n][0], len(stages[n])), pl.ds(p * width, width)
        await_bytes(main.at[pl.ds(0, 2 * HALO), here, there], s_recv.at[n * parts + p])

    def stencil(b):
        held = pl.ds(pl.multiple_of(b * block, block), block)
        late = jnp.maximum(b - halves, 0)
        turn_of = lax.rem(late, nd - 1)
        k = jnp.where(b < halves, 0, jnp.where(turn_of == 0, 1, jnp.where(turn_of == 1, nd - 1, turn_of)))
        h = jnp.where(b < halves, b, late // (nd - 1))
        of_owner = pl.ds(pl.multiple_of(h * block, block), block)
        base = lax.rem(d + nd - k, nd) * group + h * block
        here = pl.ds(pl.multiple_of(base, block), block)

        first, last = lane == 0, lane == 127

        def cut(row):
            return [row[:, 128 * t : 128 * t + 128] for t in range(tiles)]

        def raw(e, part):
            if e < HALO:
                side, r = 0, rows - HALO + e
            elif e < HALO + rows:
                side, r = 1, e - HALO
            else:
                side, r = 2, e - HALO - rows
            beside = pltpu.roll(halos[side, k, of_owner, :].astype(F32)[part], (128 - 8 * r - HALO) % 128, 1)
            row = cut(main[e, held, :].astype(F32)[part]) + [jnp.where(edge, beside, 0.0)]
            if side == 0:
                row = [jnp.where(s > 0, v, 0.0) for v in row]
            if side == 2:
                row = [jnp.where(s < ns - 1, v, 0.0) for v in row]
            return row

        def beside_of(row):
            next_first, next_out = pltpu.roll(row[0], 127, 1), pltpu.roll(row[tiles], 127, 1)
            last_last, last_out = pltpu.roll(row[tiles - 1], 1, 1), pltpu.roll(row[tiles], 1, 1)
            right = row[1:tiles] + [jnp.where(last, next_out, next_first), jnp.where(last, next_first, next_out)]
            left = [jnp.where(first, last_out, last_last)] + row[0 : tiles - 1] + [jnp.where(first, last_last, last_out)]
            return [a + b for a, b in zip(left, right)]

        def of_row(n, j):
            row = coef[n, j : j + 1]
            return cut(row) + [row[:, quarter:wide]]

        def around(rows_of, j, own):
            return [
                (a + b) + (n + w * v)
                for a, b, n, w, v in zip(rows_of[j - 1], rows_of[j + 1], beside_of(rows_of[j]), own, rows_of[j])]

        def times(a, b):
            return [v * w for v, w in zip(a, b)]

        six = [6.0] * (tiles + 1)
        for start in range(0, block, 8):
            part = slice(start, start + 8)
            field, state, flux, source = {}, {}, {}, {}
            for e in range(ext):
                field[e] = raw(e, part)
                j = e - 1
                if j >= 1:
                    state[j] = times(of_row(0, j), around(field, j, six))
                j = e - 2
                if j >= 2:
                    flux[j] = times(of_row(2, j), around(state, j, of_row(1, j)))
                j = e - 3
                if j >= 3:
                    source[j] = times(of_row(0, j), around(flux, j, of_row(1, j)))
                j = e - 4
                if j >= 4:
                    again = cut(main[j, held, :].astype(F32)[part])
                    value = [v + 0.1 * w for v, w in zip(again, around(source, j, six))]
                    values[j - HALO, part, :] = jnp.concatenate(value, axis=1)
        for r in range(rows):
            high, low = split(values[r])
            both[r, here, :] = high
            both[r, pl.ds(pl.multiple_of(dirs + base, block), block), :] = low

    before = {b: [] for b in range(len(blocks))}

    def await_own():
        await_bytes(main.at[pl.ds(0, 2 * HALO), pl.ds(0, halves * block), :], own_recv.at[0])
        await_bytes(halos.at[pl.ds(0, 2)], pack_recv.at[1])

    for i, round_stages in enumerate(rounds):
        for p in range(parts):
            for n in round_stages:
                before[i * parts + p].append(functools.partial(forward, n, p))
    before[0].append(await_own)
    for n, stage in enumerate(stages):
        for p in range(parts):
            before[stage[0]].append(functools.partial(await_rows, n, p))

    def step(b, carry):
        for at, actions in before.items():
            if actions:
                @pl.when(b == at)
                def _():
                    for action in actions:
                        action()
        stencil(b)
        return carry

    lax.fori_loop(0, len(blocks), step, 0)

    total = nt_dot(both[0], both[0])
    for r in range(1, rows):
        total = total + nt_dot(both[r], both[r])
    gram[...] = total
    mixed = gram[0:dirs, dirs : 2 * dirs] + gram[dirs : 2 * dirs, 0:dirs]
    local = (gram[0:dirs, 0:dirs] + gram[dirs : 2 * dirs, dirs : 2 * dirs] + mixed) * (1.0 / total_cells)
    result[...] = local.reshape(na, tile, dirs)

    for offset in off_a:
        i, peer = at_a(offset)
        send(result.at[i], part.at[ia], 6, g_recv.at[0], peer)
    part[ia] = result[ia]

    deal[...] = (lax.rem(line, 128) * tiles + line // 128 == spot).astype(F32).astype(BF16)

    def undeal(r, carry):
        both[r] = nn_dot(both[r], deal[...]).astype(BF16)
        return carry

    lax.fori_loop(0, rows, undeal, 0)
    await_bytes(part.at[pl.ds(0, na - 1)], g_recv.at[0])
    part_b[ib] = jnp.sum(part[...], axis=0)
    for offset in off_b:
        send(part_b.at[ib], part_b.at[ib], 7, g_recv.at[1], at_b(offset))
    await_bytes(part_b.at[pl.ds(0, nb - 1)], g_recv.at[1])
    part_c[ia] = jnp.sum(part_b[...], axis=0)
    for offset in off_a:
        send(part_c.at[ia], part_c.at[ia], 8, g_recv.at[2], at_a(offset)[1])
    await_bytes(part_c.at[pl.ds(0, na - 1)], g_recv.at[2])

    whole = part_c[...].reshape(dirs, dirs)
    upper, inverse = factor_and_inverse([whole[t : t + 8] for t in range(0, dirs, 8)])
    factor_ref[...] = upper
    inverse_high, inverse_low = split(inverse)
    inverse_twice = jnp.concatenate([inverse_high, inverse_high], axis=1)

    step_rows = 2
    turned_out = main.at[pl.ds(0, rows)]
    await_bytes(main.at[:, pl.ds(0, (nd - 1) * block), :], sends.at[5])

    def basis_step(j, carry):
        for t in range(step_rows):
            r = j * step_rows + t
            value = nn_dot(inverse_twice, both[r]) + nn_dot(inverse_low, both[r, 0:dirs, :])
            turned_out[r] = value.astype(BF16)
        for k in list(range(2, nd)) + [1]:
            q = lax.rem(d + k, nd)
            here = pl.ds(j * step_rows, step_rows)
            send(turned_out.at[here, dirs_at(q), :], out_ref.at[here, :, cols_at(d)], 9, o_recv.at[0], {"space": s, "dir": q})
        return carry

    lax.fori_loop(0, rows // step_rows, basis_step, 0)
    own_out = pltpu.make_async_copy(turned_out.at[:, dirs_at(d), :], out_ref.at[:, :, cols_at(d)], own_sem.at[1])
    own_out.start()
    await_bytes(halos.at[1, pl.ds(0, nd - 1)], sends.at[0])
    await_bytes(coef_in, sends.at[1])
    await_bytes(main.at[pl.ds(0, 2 * HALO), pl.ds(0, halves * block), :], sends.at[2])
    await_bytes(turned.at[:, :, pl.ds(0, (nd - 1) * quarter)], sends.at[3])
    await_bytes(halos.at[pl.ds(0, 2)], sends.at[4])
    await_bytes(part.at[pl.ds(0, na - 1)], sends.at[6])
    await_bytes(part_b.at[pl.ds(0, nb - 1)], sends.at[7])
    await_bytes(part_c.at[pl.ds(0, na - 1)], sends.at[8])
    own_out.wait()
    away = pl.ds(0, (nd - 1) * quarter)
    await_bytes(out_ref.at[:, :, away], o_recv.at[0])
    await_bytes(out_ref.at[:, :, away], sends.at[9])


def order_kernel(in_ref, factor_in, out_hbm, factor_out, ordered, out_sem, factor_sem):
    count = out_sem.shape[0]
    chunk = in_ref.shape[2] // count
    factor_copy = pltpu.make_async_copy(factor_in, factor_out, factor_sem.at[0])
    factor_copy.start()
    out = []
    for i in range(count):
        here = slice(i * chunk, (i + 1) * chunk)
        ordered[:, :, here] = jnp.swapaxes(in_ref[:, :, here].astype(F32), 0, 1).astype(BF16)
        there = pl.ds(i * chunk, chunk)
        out.append(pltpu.make_async_copy(ordered.at[:, :, there], out_hbm.at[:, :, there], out_sem.at[i]))
        out[i].start()
    for i in range(count):
        out[i].wait()
    factor_copy.wait()


def per_device(ns, nd, directions, depth_coef, sensitivity, obs_weight):
    group, rows, cols = directions.shape
    dirs = group * nd
    nx = 4 if ns >= 8 else ns // 2
    nz = ns // (2 * nx)
    na, nb = nx * nd, nz * 2
    tile = dirs // na
    quarter = cols // nd
    wide = quarter + 128
    ext = rows + 2 * HALO
    cfg = (nd, ns, nx, nz, rows, cols, dirs, rows * ns * cols)
    dma = pltpu.SemaphoreType.DMA
    turned, factor = pl.pallas_call(
        functools.partial(sketch_kernel, cfg),
        out_shape=(jax.ShapeDtypeStruct((rows, group, cols), BF16), jax.ShapeDtypeStruct((dirs, dirs), F32)),
        in_specs=[pl.BlockSpec(memory_space=pltpu.HBM)] * 4,
        out_specs=(pl.BlockSpec(memory_space=pltpu.VMEM),) * 2,
        scratch_shapes=[
            pltpu.VMEM((group, rows, cols), BF16),
            pltpu.VMEM((rows, cols), F32),
            pltpu.VMEM((rows, cols), F32),
            pltpu.VMEM((rows, cols), F32),
            pltpu.VMEM((rows, group, cols), BF16),
            pltpu.VMEM((nd, group, 128), BF16),
            pltpu.VMEM((ext, dirs, quarter), BF16),
            pltpu.VMEM((3, nd, group, 128), BF16),
            pltpu.VMEM((3, ext, wide), F32),
            pltpu.VMEM((3, rows, wide), F32),
            pltpu.VMEM((2, 3, rows, wide), F32),
            pltpu.VMEM((rows, 2 * dirs, quarter), BF16),
            pltpu.VMEM((rows, 16, quarter), F32),
            pltpu.VMEM((quarter, quarter), BF16),
            pltpu.VMEM((2 * dirs, 2 * dirs), F32),
            pltpu.VMEM((na, tile, dirs), F32),
            pltpu.VMEM((nb, tile, dirs), F32),
            pltpu.VMEM((na, tile, dirs), F32),
            pltpu.VMEM((na, tile, dirs), F32),
            dma((10,)), dma((8,)), dma((8,)), dma((2,)), dma((1,)), dma((1,)), dma((3,)), dma((1,)), dma((3,)), dma((4,)),
        ],
        compiler_params=pltpu.CompilerParams(collective_id=0, has_side_effects=True, vmem_limit_bytes=40 * 2**20),
    )(*(pltpu.with_memory_space_constraint(x, pltpu.HBM) for x in (directions, depth_coef, sensitivity, obs_weight)))
    return pl.pallas_call(
        order_kernel,
        out_shape=(jax.ShapeDtypeStruct((group, rows, cols), BF16), jax.ShapeDtypeStruct((dirs, dirs), F32)),
        in_specs=[pl.BlockSpec(memory_space=pltpu.VMEM)] * 2,
        out_specs=(pl.BlockSpec(memory_space=pltpu.HBM),) * 2,
        scratch_shapes=[pltpu.VMEM((group, rows, cols), BF16), dma((4,)), dma((1,))],
        compiler_params=pltpu.CompilerParams(vmem_limit_bytes=40 * 2**20),
    )(turned, factor)


def solution(mesh):
    return jax.shard_map(
        functools.partial(per_device, mesh.shape["space"], mesh.shape["dir"]),
        mesh=mesh,
        in_specs=(P("dir", "space", None), P("space", None), P("space", None), P("space", None)),
        out_specs=(P("dir", "space", None), P()),
        check_vma=False,
    )
```

```python
import functools

import jax
import jax.numpy as jnp
from jax import lax
from jax.experimental import pallas as pl
from jax.experimental.pallas import tpu as pltpu
from jax.sharding import PartitionSpec as P

MESH = pl.DeviceIdType.MESH
F32 = jnp.float32
BF16 = jnp.bfloat16
HALO = 4


def nt_dot(a, b):
    return lax.dot_general(a, b, (((1,), (1,)), ((), ())), preferred_element_type=F32)


def nn_dot(a, b):
    return lax.dot_general(a, b, (((1,), (0,)), ((), ())), preferred_element_type=F32)


def split(x):
    high = x.astype(BF16)
    return high, (x - high.astype(F32)).astype(BF16)


def tree_sum(terms):
    terms = list(terms)
    while len(terms) > 1:
        terms = [terms[i] + terms[i + 1] if i + 1 < len(terms) else terms[i] for i in range(0, len(terms), 2)]
    return terms[0]


def factor_and_inverse(tiles):
    size = 8 * len(tiles)
    tiles = list(tiles)

    def spread(v):
        return jnp.broadcast_to(v, (8, size))

    lane = lax.broadcasted_iota(jnp.int32, (8, size), 1)
    sub = lax.broadcasted_iota(jnp.int32, (8, size), 0)
    upper, inverse = [], []
    for p in range(len(tiles)):
        x, o = tiles[p], 8 * p
        columns = [spread(x[:, o + j : o + j + 1]) for j in range(8)]
        e = {(i, j): spread(columns[j][i : i + 1]) for j in range(8) for i in range(j, 8)}
        r, l, f, unit, w = [], {}, {}, {}, {}
        for j in range(8):
            over = 1.0 / e[j, j]
            r.append(lax.rsqrt(e[j, j]))
            for i in range(j + 1, 8):
                f[i, j] = e[i, j] * over
                l[i, j] = e[i, j] * r[j]
            for i in range(j + 1, 8):
                for k in range(j + 1, i + 1):
                    e[i, k] = e[i, k] - (e[i, j] * e[k, j]) * over
        for j in range(8):
            for i in range(j + 1, 8):
                unit[i, j] = -tree_sum([f[i, j]] + [f[i, k] * unit[k, j] for k in range(j + 1, i)])
        for j in range(8):
            w[j, j] = r[j]
            for i in range(j + 1, 8):
                w[i, j] = r[i] * unit[i, j]
        panel = (lane >= o) & (lane < o + 8)
        rows = [spread(v) for v in jnp.split(jnp.where(panel, jnp.where(lane - o == sub, 1.0, 0.0), x), 8, axis=0)]
        solved = [tree_sum([w[j, i] * rows[i] for i in range(j + 1)]) for j in range(8)]
        scaled = [tree_sum([w[j, i] * solved[j] for j in range(i, 8)]) for i in range(8)]
        for t in range(p + 1, len(tiles)):
            taken = tree_sum([spread(tiles[t][:, o + j : o + j + 1]) * scaled[j] for j in range(8)])
            tiles[t] = jnp.where(panel, 0.0, tiles[t]) - taken
        below = solved[0]
        for j in range(1, 8):
            below = jnp.where(sub == j, solved[j], below)
        above = below
        for j in range(8):
            for i in range(j, 8):
                above = jnp.where((sub == j) & (lane == o + i), e[j, j] * r[j] if i == j else l[i, j], above)
        inverse.append(jnp.where(lane < o + 8, below, 0.0))
        upper.append(jnp.where(lane >= o + sub, above, 0.0))
    return jnp.concatenate(upper, axis=0), jnp.concatenate(inverse, axis=0)


def sketch_kernel(
    cfg, dirs_hbm, depth_hbm, sens_hbm, obs_hbm, out_ref, factor_ref,
    dirs_ref, depth_ref, sens_ref, obs_ref, turned, packs, main, halos, coef, coef_own, coef_in, both, values, deal, gram, part, part_b, part_c, result,
    sends, y_recv, s_recv, pack_recv, own_recv, c_recv, g_recv, o_recv, own_sem, in_sem,
):
    nd, ns, nx, nz, rows, cols, dirs, total_cells = cfg
    quarter = cols // nd
    wide = quarter + 128
    group = dirs // nd
    ext = rows + 2 * HALO
    na, nb = nx * nd, nz * 2
    tile = dirs // na

    s = lax.axis_index("space")
    d = lax.axis_index("dir")
    z, x, c = s // (2 * nx), (s // 2) % nx, s % 2
    ia = x * nd + d
    ib = z * 2 + c
    down, up = lax.rem(s + ns - 1, ns), lax.rem(s + 1, ns)

    def far(offset, length):
        return min(offset, length - offset)

    off_a = sorted(((i, j) for i in range(nx) for j in range(nd)), key=lambda o: -far(o[0], nx) - far(o[1], nd))[:-1]
    off_b = sorted(((i, j) for i in range(nz) for j in range(2)), key=lambda o: -2 * far(o[0], nz) - o[1])[:-1]

    def at_a(offset):
        i, j = lax.rem(x + offset[0], nx), lax.rem(d + offset[1], nd)
        return i * nd + j, {"space": (z * nx + i) * 2 + c, "dir": j}

    def at_b(offset):
        return {"space": (lax.rem(z + offset[0], nz) * nx + x) * 2 + lax.rem(c + offset[1], 2), "dir": d}

    def send(source, target, number, arrival, peer):
        pltpu.make_async_remote_copy(
            src_ref=source, dst_ref=target, send_sem=sends.at[number], recv_sem=arrival,
            device_id=peer, device_id_type=MESH).start()

    def await_bytes(ref, sem):
        pltpu.make_async_copy(ref, ref, sem).wait()

    inputs = [
        pltpu.make_async_copy(source, target, in_sem.at[i])
        for i, (source, target) in enumerate(
            ((dirs_hbm, dirs_ref), (depth_hbm, depth_ref), (sens_hbm, sens_ref), (obs_hbm, obs_ref)))
    ]
    for copy in inputs:
        copy.start()

    barrier = pltpu.get_barrier_semaphore()
    peers = [{"space": s, "dir": lax.rem(d + k, nd)} for k in range(1, nd)]
    peers += [{"space": down, "dir": d}, {"space": up, "dir": d}]
    peers += [{"space": (z * nx + lax.rem(x + k, nx)) * 2 + c, "dir": d} for k in range(1, nx)]
    peers += [{"space": (lax.rem(z + k, nz) * nx + x) * 2 + c, "dir": d} for k in range(1, nz)]
    for peer in peers:
        pl.semaphore_signal(barrier, inc=1, device_id=peer, device_id_type=MESH)

    lane = lax.broadcasted_iota(jnp.int32, (1, 128), 1)
    edge = (lane < HALO) | (lane >= 128 - HALO)

    tiles = quarter // 128
    line = lax.broadcasted_iota(jnp.int32, (quarter, quarter), 0)
    spot = lax.broadcasted_iota(jnp.int32, (quarter, quarter), 1)
    deal[...] = (lax.rem(spot, 128) * tiles + spot // 128 == line).astype(F32).astype(BF16)

    inputs[0].wait()

    def turn(q, carry):
        here = pl.ds(pl.multiple_of(q * quarter, quarter), quarter)
        dealt = nn_dot(dirs_ref[:, :, here].astype(F32).reshape(group * rows, quarter).astype(BF16), deal[...])
        turned[:, :, here] = jnp.swapaxes(dealt.reshape(group, rows, quarter), 0, 1).astype(BF16)
        return carry

    lax.fori_loop(0, nd, turn, 0)

    for q in range(nd):
        def by_row(start, there):
            return jnp.swapaxes(dirs_ref[:, :, start : start + 128].astype(F32), 0, 1) if there else jnp.zeros((rows, group, 128), F32)

        beside = jnp.where(lane < 64, by_row((q + 1) * quarter, q < nd - 1), by_row(q * quarter - 128, q > 0))
        packed = jnp.zeros((group, 128), F32)
        for r in range(rows):
            packed = jnp.where((lane >= 8 * r) & (lane < 8 * r + 8), pltpu.roll(beside[r], 8 * r + HALO, 1), packed)
        packs[q] = packed.astype(BF16)

    for copy in inputs[1:]:
        copy.wait()
    inner = pl.ds(pl.multiple_of(d * quarter, 128), quarter)
    after = pl.ds(pl.multiple_of(jnp.minimum((d + 1) * quarter, cols - 128), 128), 128)
    before = pl.ds(pl.multiple_of(jnp.maximum(d * quarter - 128, 0), 128), 128)
    valid = ((lane < HALO) & (d < nd - 1)) | ((lane >= 128 - HALO) & (d > 0))

    def quarter_of(ref):
        return jnp.concatenate([ref[:, inner], jnp.where(lane < 64, ref[:, after], ref[:, before])], axis=1)

    inside = jnp.concatenate([jnp.ones((1, quarter), jnp.bool_), valid], axis=1)
    depth = quarter_of(depth_ref)
    coef_own[0] = jnp.where(inside, 0.1 * quarter_of(sens_ref), 0.0)
    coef_own[1] = jnp.where(inside, 20.0 / depth - 4.0, 0.0)
    coef_own[2] = jnp.where(inside, 0.1 * depth * depth * quarter_of(obs_ref), 0.0)

    pl.semaphore_wait(barrier, len(peers))

    above, below = {"space": up, "dir": d}, {"space": down, "dir": d}
    block = 16
    halves = group // block

    def dirs_at(g):
        return pl.ds(pl.multiple_of(g * group, group), group)

    def cols_at(q):
        return pl.ds(pl.multiple_of(q * quarter, 128), quarter)

    owners = [1, nd - 1] + list(range(2, nd - 1))
    blocks = [(0, h) for h in range(halves)] + [(k, h) for h in range(halves) for k in owners]
    final = len(blocks) - len(owners)
    stages = [list(range(b, b + len(owners))) for b in range(halves, final, len(owners))] + [[b] for b in range(final, len(blocks))]
    whole_stages = len(stages) - len(owners)
    parts = 1
    width = quarter // parts

    def place(b, count=1):
        return pl.ds(b * block, count * block)

    own_copies = [pltpu.make_async_copy(packs.at[d], halos.at[1, 0], own_sem.at[0])]
    for h in range(halves):
        own_copies.append(pltpu.make_async_copy(
            turned.at[:, pl.ds(h * block, block), cols_at(d)], main.at[pl.ds(HALO, rows), place(h), :], own_sem.at[1 + h]))
    for copy in own_copies:
        copy.start()
    for k in range(1, nd):
        q = lax.rem(d + k, nd)
        send(packs.at[q], halos.at[1, k], 0, pack_recv.at[0], {"space": s, "dir": q})
    for side, peer in enumerate((above, below)):
        send(coef_own, coef_in.at[side], 1, c_recv.at[0], peer)
    for h in range(halves):
        here = pl.ds(h * block, block)
        send(turned.at[pl.ds(rows - HALO, HALO), here, cols_at(d)], main.at[pl.ds(0, HALO), place(h), :], 2, own_recv.at[0], above)
        send(turned.at[pl.ds(0, HALO), here, cols_at(d)], main.at[pl.ds(HALO + rows, HALO), place(h), :], 2, own_recv.at[0], below)
    rounds = [[n] for n in range(whole_stages)] + [list(range(whole_stages, len(stages)))]
    for round_stages in rounds:
        for p in range(parts):
            pieces = [(n, b) for n in round_stages for b in stages[n]]
            for n, b in pieces[2:] + pieces[:2]:
                k, h = blocks[b]
                q = lax.rem(d + k, nd)
                there = pl.ds(pl.multiple_of(q * quarter + p * width, 128), width)
                send(turned.at[:, pl.ds(h * block, block), there],
                     main.at[pl.ds(HALO, rows), place(b), pl.ds(p * width, width)],
                     3, y_recv.at[n * parts + p], {"space": s, "dir": q})
    for copy in own_copies:
        copy.wait()

    await_bytes(coef_in, c_recv.at[0])
    for i in range(3):
        coef[i, HALO : HALO + rows] = coef_own[i]
        coef[i, 0:HALO] = jnp.where(s > 0, coef_in[0, i, rows - HALO : rows], 0.0)
        coef[i, HALO + rows : ext] = jnp.where(s < ns - 1, coef_in[1, i, 0:HALO], 0.0)
        plain = coef[i, :, 0:quarter]
        high = plain.astype(BF16)
        middle, low = split(plain - high.astype(F32))
        dealt = nn_dot(jnp.concatenate([high, middle, low], axis=0), deal[...])
        coef[i, :, 0:quarter] = (dealt[0:ext] + dealt[ext : 2 * ext]) + dealt[2 * ext : 3 * ext]

    await_bytes(halos.at[1, pl.ds(0, nd - 1)], pack_recv.at[0])
    for side, peer in enumerate((above, below)):
        send(halos.at[1], halos.at[2 * side], 4, pack_recv.at[1], peer)

    def forward(n, p):
        here, there = place(stages[n][0], len(stages[n])), pl.ds(p * width, width)
        number = n * parts + p
        await_bytes(main.at[pl.ds(0, rows), here, there], y_recv.at[number])
        send(main.at[pl.ds(rows, HALO), here, there], main.at[pl.ds(0, HALO), here, there], 5, s_recv.at[number], above)
        send(main.at[pl.ds(HALO, HALO), here, there], main.at[pl.ds(HALO + rows, HALO), here, there], 5, s_recv.at[number], below)

    def await_rows(n, p):
        here, there = place(stages[n][0], len(stages[n])), pl.ds(p * width, width)
        await_bytes(main.at[pl.ds(0, 2 * HALO), here, there], s_recv.at[n * parts + p])

    def stencil(b):
        held = pl.ds(pl.multiple_of(b * block, block), block)
        late = jnp.maximum(b - halves, 0)
        turn_of = lax.rem(late, nd - 1)
        k = jnp.where(b < halves, 0, jnp.where(turn_of == 0, 1, jnp.where(turn_of == 1, nd - 1, turn_of)))
        h = jnp.where(b < halves, b, late // (nd - 1))
        of_owner = pl.ds(pl.multiple_of(h * block, block), block)
        base = lax.rem(d + nd - k, nd) * group + h * block
        here = pl.ds(pl.multiple_of(base, block), block)

        first, last = lane == 0, lane == 127

        def cut(row):
            return [row[:, 128 * t : 128 * t + 128] for t in range(tiles)]

        def raw(e, part):
            if e < HALO:
                side, r = 0, rows - HALO + e
            elif e < HALO + rows:
                side, r = 1, e - HALO
            else:
                side, r = 2, e - HALO - rows
            beside = pltpu.roll(halos[side, k, of_owner, :].astype(F32)[part], (128 - 8 * r - HALO) % 128, 1)
            row = cut(main[e, held, :].astype(F32)[part]) + [jnp.where(edge, beside, 0.0)]
            if side == 0:
                row = [jnp.where(s > 0, v, 0.0) for v in row]
            if side == 2:
                row = [jnp.where(s < ns - 1, v, 0.0) for v in row]
            return row

        def beside_of(row):
            next_first, next_out = pltpu.roll(row[0], 127, 1), pltpu.roll(row[tiles], 127, 1)
            last_last, last_out = pltpu.roll(row[tiles - 1], 1, 1), pltpu.roll(row[tiles], 1, 1)
            right = row[1:tiles] + [jnp.where(last, next_out, next_first), jnp.where(last, next_first, next_out)]
            left = [jnp.where(first, last_out, last_last)] + row[0 : tiles - 1] + [jnp.where(first, last_last, last_out)]
            return [a + b for a, b in zip(left, right)]

        def of_row(n, j):
            row = coef[n, j : j + 1]
            return cut(row) + [row[:, quarter:wide]]

        def around(rows_of, j, own):
            return [
                (a + b) + (n + w * v)
                for a, b, n, w, v in zip(rows_of[j - 1], rows_of[j + 1], beside_of(rows_of[j]), own, rows_of[j])]

        def times(a, b):
            return [v * w for v, w in zip(a, b)]

        six = [6.0] * (tiles + 1)
        for start in range(0, block, 8):
            part = slice(start, start + 8)
            field, state, flux, source = {}, {}, {}, {}
            for e in range(ext):
                field[e] = raw(e, part)
                j = e - 1
                if j >= 1:
                    state[j] = times(of_row(0, j), around(field, j, six))
                j = e - 2
                if j >= 2:
                    flux[j] = times(of_row(2, j), around(state, j, of_row(1, j)))
                j = e - 3
                if j >= 3:
                    source[j] = times(of_row(0, j), around(flux, j, of_row(1, j)))
                j = e - 4
                if j >= 4:
                    again = cut(main[j, held, :].astype(F32)[part])
                    value = [v + 0.1 * w for v, w in zip(again, around(source, j, six))]
                    values[j - HALO, part, :] = jnp.concatenate(value, axis=1)
        for r in range(rows):
            high, low = split(values[r])
            both[r, here, :] = high
            both[r, pl.ds(pl.multiple_of(dirs + base, block), block), :] = low

    before = {b: [] for b in range(len(blocks))}

    def await_own():
        await_bytes(main.at[pl.ds(0, 2 * HALO), pl.ds(0, halves * block), :], own_recv.at[0])
        await_bytes(halos.at[pl.ds(0, 2)], pack_recv.at[1])

    for i, round_stages in enumerate(rounds):
        for p in range(parts):
            for n in round_stages:
                before[i * parts + p].append(functools.partial(forward, n, p))
    before[0].append(await_own)
    for n, stage in enumerate(stages):
        for p in range(parts):
            before[stage[0]].append(functools.partial(await_rows, n, p))

    def step(b, carry):
        for at, actions in before.items():
            if actions:
                @pl.when(b == at)
                def _():
                    for action in actions:
                        action()
        stencil(b)
        return carry

    lax.fori_loop(0, len(blocks), step, 0)

    total = nt_dot(both[0], both[0])
    for r in range(1, rows):
        total = total + nt_dot(both[r], both[r])
    gram[...] = total
    mixed = gram[0:dirs, dirs : 2 * dirs] + gram[dirs : 2 * dirs, 0:dirs]
    local = (gram[0:dirs, 0:dirs] + gram[dirs : 2 * dirs, dirs : 2 * dirs] + mixed) * (1.0 / total_cells)
    result[...] = local.reshape(na, tile, dirs)

    for offset in off_a:
        i, peer = at_a(offset)
        send(result.at[i], part.at[ia], 6, g_recv.at[0], peer)
    part[ia] = result[ia]

    deal[...] = (lax.rem(line, 128) * tiles + line // 128 == spot).astype(F32).astype(BF16)

    def undeal(r, carry):
        both[r] = nn_dot(both[r], deal[...]).astype(BF16)
        return carry

    lax.fori_loop(0, rows, undeal, 0)
    await_bytes(part.at[pl.ds(0, na - 1)], g_recv.at[0])
    part_b[ib] = jnp.sum(part[...], axis=0)
    for offset in off_b:
        send(part_b.at[ib], part_b.at[ib], 7, g_recv.at[1], at_b(offset))
    await_bytes(part_b.at[pl.ds(0, nb - 1)], g_recv.at[1])
    part_c[ia] = jnp.sum(part_b[...], axis=0)
    for offset in off_a:
        send(part_c.at[ia], part_c.at[ia], 8, g_recv.at[2], at_a(offset)[1])
    await_bytes(part_c.at[pl.ds(0, na - 1)], g_recv.at[2])

    whole = part_c[...].reshape(dirs, dirs)
    upper, inverse = factor_and_inverse([whole[t : t + 8] for t in range(0, dirs, 8)])
    factor_ref[...] = upper
    inverse_high, inverse_low = split(inverse)
    inverse_twice = jnp.concatenate([inverse_high, inverse_high], axis=1)

    step_rows = 2
    turned_out = main.at[pl.ds(0, rows)]
    await_bytes(main.at[:, pl.ds(0, (nd - 1) * block), :], sends.at[5])

    def basis_step(j, carry):
        for t in range(step_rows):
            r = j * step_rows + t
            value = nn_dot(inverse_twice, both[r]) + nn_dot(inverse_low, both[r, 0:dirs, :])
            turned_out[r] = value.astype(BF16)
        for k in list(range(2, nd)) + [1]:
            q = lax.rem(d + k, nd)
            here = pl.ds(j * step_rows, step_rows)
            send(turned_out.at[here, dirs_at(q), :], out_ref.at[here, :, cols_at(d)], 9, o_recv.at[0], {"space": s, "dir": q})
        return carry

    lax.fori_loop(0, rows // step_rows, basis_step, 0)
    own_out = pltpu.make_async_copy(turned_out.at[:, dirs_at(d), :], out_ref.at[:, :, cols_at(d)], own_sem.at[1])
    own_out.start()
    await_bytes(halos.at[1, pl.ds(0, nd - 1)], sends.at[0])
    await_bytes(coef_in, sends.at[1])
    await_bytes(main.at[pl.ds(0, 2 * HALO), pl.ds(0, halves * block), :], sends.at[2])
    await_bytes(turned.at[:, :, pl.ds(0, (nd - 1) * quarter)], sends.at[3])
    await_bytes(halos.at[pl.ds(0, 2)], sends.at[4])
    await_bytes(part.at[pl.ds(0, na - 1)], sends.at[6])
    await_bytes(part_b.at[pl.ds(0, nb - 1)], sends.at[7])
    await_bytes(part_c.at[pl.ds(0, na - 1)], sends.at[8])
    own_out.wait()
    away = pl.ds(0, (nd - 1) * quarter)
    await_bytes(out_ref.at[:, :, away], o_recv.at[0])
    await_bytes(out_ref.at[:, :, away], sends.at[9])


def order_kernel(in_ref, factor_in, out_hbm, factor_out, ordered, out_sem, factor_sem):
    count = out_sem.shape[0]
    chunk = in_ref.shape[2] // count
    factor_copy = pltpu.make_async_copy(factor_in, factor_out, factor_sem.at[0])
    factor_copy.start()
    out = []
    for i in range(count):
        here = slice(i * chunk, (i + 1) * chunk)
        ordered[:, :, here] = jnp.swapaxes(in_ref[:, :, here].astype(F32), 0, 1).astype(BF16)
        there = pl.ds(i * chunk, chunk)
        out.append(pltpu.make_async_copy(ordered.at[:, :, there], out_hbm.at[:, :, there], out_sem.at[i]))
        out[i].start()
    for i in range(count):
        out[i].wait()
    factor_copy.wait()


def per_device(ns, nd, directions, depth_coef, sensitivity, obs_weight):
    group, rows, cols = directions.shape
    dirs = group * nd
    nx = 4 if ns >= 8 else ns // 2
    nz = ns // (2 * nx)
    na, nb = nx * nd, nz * 2
    tile = dirs // na
    quarter = cols // nd
    wide = quarter + 128
    ext = rows + 2 * HALO
    cfg = (nd, ns, nx, nz, rows, cols, dirs, rows * ns * cols)
    dma = pltpu.SemaphoreType.DMA
    turned, factor = pl.pallas_call(
        functools.partial(sketch_kernel, cfg),
        out_shape=(jax.ShapeDtypeStruct((rows, group, cols), BF16), jax.ShapeDtypeStruct((dirs, dirs), F32)),
        in_specs=[pl.BlockSpec(memory_space=pltpu.HBM)] * 4,
        out_specs=(pl.BlockSpec(memory_space=pltpu.VMEM),) * 2,
        scratch_shapes=[
            pltpu.VMEM((group, rows, cols), BF16),
            pltpu.VMEM((rows, cols), F32),
            pltpu.VMEM((rows, cols), F32),
            pltpu.VMEM((rows, cols), F32),
            pltpu.VMEM((rows, group, cols), BF16),
            pltpu.VMEM((nd, group, 128), BF16),
            pltpu.VMEM((ext, dirs, quarter), BF16),
            pltpu.VMEM((3, nd, group, 128), BF16),
            pltpu.VMEM((3, ext, wide), F32),
            pltpu.VMEM((3, rows, wide), F32),
            pltpu.VMEM((2, 3, rows, wide), F32),
            pltpu.VMEM((rows, 2 * dirs, quarter), BF16),
            pltpu.VMEM((rows, 16, quarter), F32),
            pltpu.VMEM((quarter, quarter), BF16),
            pltpu.VMEM((2 * dirs, 2 * dirs), F32),
            pltpu.VMEM((na, tile, dirs), F32),
            pltpu.VMEM((nb, tile, dirs), F32),
            pltpu.VMEM((na, tile, dirs), F32),
            pltpu.VMEM((na, tile, dirs), F32),
            dma((10,)), dma((8,)), dma((8,)), dma((2,)), dma((1,)), dma((1,)), dma((3,)), dma((1,)), dma((3,)), dma((4,)),
        ],
        compiler_params=pltpu.CompilerParams(collective_id=0, has_side_effects=True, vmem_limit_bytes=40 * 2**20),
    )(*(pltpu.with_memory_space_constraint(x, pltpu.HBM) for x in (directions, depth_coef, sensitivity, obs_weight)))
    return pl.pallas_call(
        order_kernel,
        out_shape=(jax.ShapeDtypeStruct((group, rows, cols), BF16), jax.ShapeDtypeStruct((dirs, dirs), F32)),
        in_specs=[pl.BlockSpec(memory_space=pltpu.VMEM)] * 2,
        out_specs=(pl.BlockSpec(memory_space=pltpu.HBM),) * 2,
        scratch_shapes=[pltpu.VMEM((group, rows, cols), BF16), dma((4,)), dma((1,))],
        compiler_params=pltpu.CompilerParams(vmem_limit_bytes=40 * 2**20),
    )(turned, factor)


def solution(mesh):
    return jax.shard_map(
        functools.partial(per_device, mesh.shape["space"], mesh.shape["dir"]),
        mesh=mesh,
        in_specs=(P("dir", "space", None), P("space", None), P("space", None), P("space", None)),
        out_specs=(P("dir", "space", None), P()),
        check_vma=False,
    )
```

```python
import functools

import jax
import jax.numpy as jnp
from jax import lax
from jax.experimental import pallas as pl
from jax.experimental.pallas import tpu as pltpu
from jax.sharding import PartitionSpec as P

MESH = pl.DeviceIdType.MESH
F32 = jnp.float32
BF16 = jnp.bfloat16
HALO = 4


def nt_dot(a, b):
    return lax.dot_general(a, b, (((1,), (1,)), ((), ())), preferred_element_type=F32)


def nn_dot(a, b):
    return lax.dot_general(a, b, (((1,), (0,)), ((), ())), preferred_element_type=F32)


def split(x):
    high = x.astype(BF16)
    return high, (x - high.astype(F32)).astype(BF16)


def tree_sum(terms):
    terms = list(terms)
    while len(terms) > 1:
        terms = [terms[i] + terms[i + 1] if i + 1 < len(terms) else terms[i] for i in range(0, len(terms), 2)]
    return terms[0]


def factor_and_inverse(tiles):
    size = 8 * len(tiles)
    tiles = list(tiles)

    def spread(v):
        return jnp.broadcast_to(v, (8, size))

    lane = lax.broadcasted_iota(jnp.int32, (8, size), 1)
    sub = lax.broadcasted_iota(jnp.int32, (8, size), 0)
    upper, inverse = [], []
    for p in range(len(tiles)):
        x, o = tiles[p], 8 * p
        columns = [spread(x[:, o + j : o + j + 1]) for j in range(8)]
        e = {(i, j): spread(columns[j][i : i + 1]) for j in range(8) for i in range(j, 8)}
        r, l, f, unit, w = [], {}, {}, {}, {}
        for j in range(8):
            over = 1.0 / e[j, j]
            r.append(lax.rsqrt(e[j, j]))
            for i in range(j + 1, 8):
                f[i, j] = e[i, j] * over
                l[i, j] = e[i, j] * r[j]
            for i in range(j + 1, 8):
                for k in range(j + 1, i + 1):
                    e[i, k] = e[i, k] - (e[i, j] * e[k, j]) * over
        for j in range(8):
            for i in range(j + 1, 8):
                unit[i, j] = -tree_sum([f[i, j]] + [f[i, k] * unit[k, j] for k in range(j + 1, i)])
        for j in range(8):
            w[j, j] = r[j]
            for i in range(j + 1, 8):
                w[i, j] = r[i] * unit[i, j]
        panel = (lane >= o) & (lane < o + 8)
        rows = [spread(v) for v in jnp.split(jnp.where(panel, jnp.where(lane - o == sub, 1.0, 0.0), x), 8, axis=0)]
        solved = [tree_sum([w[j, i] * rows[i] for i in range(j + 1)]) for j in range(8)]
        scaled = [tree_sum([w[j, i] * solved[j] for j in range(i, 8)]) for i in range(8)]
        for t in range(p + 1, len(tiles)):
            taken = tree_sum([spread(tiles[t][:, o + j : o + j + 1]) * scaled[j] for j in range(8)])
            tiles[t] = jnp.where(panel, 0.0, tiles[t]) - taken
        below = solved[0]
        for j in range(1, 8):
            below = jnp.where(sub == j, solved[j], below)
        above = below
        for j in range(8):
            for i in range(j, 8):
                above = jnp.where((sub == j) & (lane == o + i), e[j, j] * r[j] if i == j else l[i, j], above)
        inverse.append(jnp.where(lane < o + 8, below, 0.0))
        upper.append(jnp.where(lane >= o + sub, above, 0.0))
    return jnp.concatenate(upper, axis=0), jnp.concatenate(inverse, axis=0)


def sketch_kernel(
    cfg, dirs_hbm, depth_hbm, sens_hbm, obs_hbm, out_ref, factor_ref,
    dirs_ref, depth_ref, sens_ref, obs_ref, turned, packs, main, halos, coef, coef_own, coef_in, both, values, deal, gram, part, part_b, part_c, result,
    sends, y_recv, s_recv, pack_recv, own_recv, c_recv, g_recv, o_recv, own_sem, in_sem,
):
    nd, ns, nx, nz, rows, cols, dirs, total_cells = cfg
    quarter = cols // nd
    wide = quarter + 128
    group = dirs // nd
    ext = rows + 2 * HALO
    na, nb = nx * nd, nz * 2
    tile = dirs // na

    s = lax.axis_index("space")
    d = lax.axis_index("dir")
    z, x, c = s // (2 * nx), (s // 2) % nx, s % 2
    ia = x * nd + d
    ib = z * 2 + c
    down, up = lax.rem(s + ns - 1, ns), lax.rem(s + 1, ns)

    def far(offset, length):
        return min(offset, length - offset)

    off_a = sorted(((i, j) for i in range(nx) for j in range(nd)), key=lambda o: -far(o[0], nx) - far(o[1], nd))[:-1]
    off_b = sorted(((i, j) for i in range(nz) for j in range(2)), key=lambda o: -2 * far(o[0], nz) - o[1])[:-1]

    def at_a(offset):
        i, j = lax.rem(x + offset[0], nx), lax.rem(d + offset[1], nd)
        return i * nd + j, {"space": (z * nx + i) * 2 + c, "dir": j}

    def at_b(offset):
        return {"space": (lax.rem(z + offset[0], nz) * nx + x) * 2 + lax.rem(c + offset[1], 2), "dir": d}

    def send(source, target, number, arrival, peer):
        pltpu.make_async_remote_copy(
            src_ref=source, dst_ref=target, send_sem=sends.at[number], recv_sem=arrival,
            device_id=peer, device_id_type=MESH).start()

    def await_bytes(ref, sem):
        pltpu.make_async_copy(ref, ref, sem).wait()

    inputs = [
        pltpu.make_async_copy(source, target, in_sem.at[i])
        for i, (source, target) in enumerate(
            ((dirs_hbm, dirs_ref), (depth_hbm, depth_ref), (sens_hbm, sens_ref), (obs_hbm, obs_ref)))
    ]
    for copy in inputs:
        copy.start()

    barrier = pltpu.get_barrier_semaphore()
    peers = [{"space": s, "dir": lax.rem(d + k, nd)} for k in range(1, nd)]
    peers += [{"space": down, "dir": d}, {"space": up, "dir": d}]
    peers += [{"space": (z * nx + lax.rem(x + k, nx)) * 2 + c, "dir": d} for k in range(1, nx)]
    peers += [{"space": (lax.rem(z + k, nz) * nx + x) * 2 + c, "dir": d} for k in range(1, nz)]
    for peer in peers:
        pl.semaphore_signal(barrier, inc=1, device_id=peer, device_id_type=MESH)

    lane = lax.broadcasted_iota(jnp.int32, (1, 128), 1)
    edge = (lane < HALO) | (lane >= 128 - HALO)

    tiles = quarter // 128
    line = lax.broadcasted_iota(jnp.int32, (quarter, quarter), 0)
    spot = lax.broadcasted_iota(jnp.int32, (quarter, quarter), 1)
    deal[...] = (lax.rem(spot, 128) * tiles + spot // 128 == line).astype(F32).astype(BF16)

    inputs[0].wait()

    def turn(q, carry):
        here = pl.ds(pl.multiple_of(q * quarter, quarter), quarter)
        dealt = nn_dot(dirs_ref[:, :, here].astype(F32).reshape(group * rows, quarter).astype(BF16), deal[...])
        turned[:, :, here] = jnp.swapaxes(dealt.reshape(group, rows, quarter), 0, 1).astype(BF16)
        return carry

    lax.fori_loop(0, nd, turn, 0)

    for q in range(nd):
        def by_row(start, there):
            return jnp.swapaxes(dirs_ref[:, :, start : start + 128].astype(F32), 0, 1) if there else jnp.zeros((rows, group, 128), F32)

        beside = jnp.where(lane < 64, by_row((q + 1) * quarter, q < nd - 1), by_row(q * quarter - 128, q > 0))
        packed = jnp.zeros((group, 128), F32)
        for r in range(rows):
            packed = jnp.where((lane >= 8 * r) & (lane < 8 * r + 8), pltpu.roll(beside[r], 8 * r + HALO, 1), packed)
        packs[q] = packed.astype(BF16)

    for copy in inputs[1:]:
        copy.wait()
    inner = pl.ds(pl.multiple_of(d * quarter, 128), quarter)
    after = pl.ds(pl.multiple_of(jnp.minimum((d + 1) * quarter, cols - 128), 128), 128)
    before = pl.ds(pl.multiple_of(jnp.maximum(d * quarter - 128, 0), 128), 128)
    valid = ((lane < HALO) & (d < nd - 1)) | ((lane >= 128 - HALO) & (d > 0))

    def quarter_of(ref):
        return jnp.concatenate([ref[:, inner], jnp.where(lane < 64, ref[:, after], ref[:, before])], axis=1)

    inside = jnp.concatenate([jnp.ones((1, quarter), jnp.bool_), valid], axis=1)
    depth = quarter_of(depth_ref)
    coef_own[0] = jnp.where(inside, 0.1 * quarter_of(sens_ref), 0.0)
    coef_own[1] = jnp.where(inside, 20.0 / depth - 4.0, 0.0)
    coef_own[2] = jnp.where(inside, 0.1 * depth * depth * quarter_of(obs_ref), 0.0)

    pl.semaphore_wait(barrier, len(peers))

    above, below = {"space": up, "dir": d}, {"space": down, "dir": d}
    block = 16
    halves = group // block

    def dirs_at(g):
        return pl.ds(pl.multiple_of(g * group, group), group)

    def cols_at(q):
        return pl.ds(pl.multiple_of(q * quarter, 128), quarter)

    owners = [1, nd - 1] + list(range(2, nd - 1))
    blocks = [(0, h) for h in range(halves)] + [(k, h) for h in range(halves) for k in owners]
    stages = [[b] for b in range(halves, len(blocks))]
    parts = 1
    width = quarter // parts

    def place(b, count=1):
        return pl.ds(b * block, count * block)

    own_copies = [pltpu.make_async_copy(packs.at[d], halos.at[1, 0], own_sem.at[0])]
    for h in range(halves):
        own_copies.append(pltpu.make_async_copy(
            turned.at[:, pl.ds(h * block, block), cols_at(d)], main.at[pl.ds(HALO, rows), place(h), :], own_sem.at[1 + h]))
    for copy in own_copies:
        copy.start()
    for k in range(1, nd):
        q = lax.rem(d + k, nd)
        send(packs.at[q], halos.at[1, k], 0, pack_recv.at[0], {"space": s, "dir": q})
    for side, peer in enumerate((above, below)):
        send(coef_own, coef_in.at[side], 1, c_recv.at[0], peer)
    for h in range(halves):
        here = pl.ds(h * block, block)
        send(turned.at[pl.ds(rows - HALO, HALO), here, cols_at(d)], main.at[pl.ds(0, HALO), place(h), :], 2, own_recv.at[0], above)
        send(turned.at[pl.ds(0, HALO), here, cols_at(d)], main.at[pl.ds(HALO + rows, HALO), place(h), :], 2, own_recv.at[0], below)
    rounds = [list(range(n, n + len(owners))) for n in range(0, len(stages), len(owners))]
    for round_stages in rounds:
        for p in range(parts):
            pieces = [(n, b) for n in round_stages for b in stages[n]]
            for n, b in pieces[2:] + pieces[:2]:
                k, h = blocks[b]
                q = lax.rem(d + k, nd)
                there = pl.ds(pl.multiple_of(q * quarter + p * width, 128), width)
                send(turned.at[:, pl.ds(h * block, block), there],
                     main.at[pl.ds(HALO, rows), place(b), pl.ds(p * width, width)],
                     3, y_recv.at[n * parts + p], {"space": s, "dir": q})
    for copy in own_copies:
        copy.wait()

    await_bytes(coef_in, c_recv.at[0])
    for i in range(3):
        coef[i, HALO : HALO + rows] = coef_own[i]
        coef[i, 0:HALO] = jnp.where(s > 0, coef_in[0, i, rows - HALO : rows], 0.0)
        coef[i, HALO + rows : ext] = jnp.where(s < ns - 1, coef_in[1, i, 0:HALO], 0.0)
        plain = coef[i, :, 0:quarter]
        high = plain.astype(BF16)
        middle, low = split(plain - high.astype(F32))
        dealt = nn_dot(jnp.concatenate([high, middle, low], axis=0), deal[...])
        coef[i, :, 0:quarter] = (dealt[0:ext] + dealt[ext : 2 * ext]) + dealt[2 * ext : 3 * ext]

    await_bytes(halos.at[1, pl.ds(0, nd - 1)], pack_recv.at[0])
    for side, peer in enumerate((above, below)):
        send(halos.at[1], halos.at[2 * side], 4, pack_recv.at[1], peer)

    def forward(n, p):
        here, there = place(stages[n][0], len(stages[n])), pl.ds(p * width, width)
        number = n * parts + p
        await_bytes(main.at[pl.ds(0, rows), here, there], y_recv.at[number])
        send(main.at[pl.ds(rows, HALO), here, there], main.at[pl.ds(0, HALO), here, there], 5, s_recv.at[number], above)
        send(main.at[pl.ds(HALO, HALO), here, there], main.at[pl.ds(HALO + rows, HALO), here, there], 5, s_recv.at[number], below)

    def await_rows(n, p):
        here, there = place(stages[n][0], len(stages[n])), pl.ds(p * width, width)
        await_bytes(main.at[pl.ds(0, 2 * HALO), here, there], s_recv.at[n * parts + p])

    def stencil(b):
        held = pl.ds(pl.multiple_of(b * block, block), block)
        late = jnp.maximum(b - halves, 0)
        turn_of = lax.rem(late, nd - 1)
        k = jnp.where(b < halves, 0, jnp.where(turn_of == 0, 1, jnp.where(turn_of == 1, nd - 1, turn_of)))
        h = jnp.where(b < halves, b, late // (nd - 1))
        of_owner = pl.ds(pl.multiple_of(h * block, block), block)
        base = lax.rem(d + nd - k, nd) * group + h * block
        here = pl.ds(pl.multiple_of(base, block), block)

        first, last = lane == 0, lane == 127

        def cut(row):
            return [row[:, 128 * t : 128 * t + 128] for t in range(tiles)]

        def raw(e, part):
            if e < HALO:
                side, r = 0, rows - HALO + e
            elif e < HALO + rows:
                side, r = 1, e - HALO
            else:
                side, r = 2, e - HALO - rows
            beside = pltpu.roll(halos[side, k, of_owner, :].astype(F32)[part], (128 - 8 * r - HALO) % 128, 1)
            row = cut(main[e, held, :].astype(F32)[part]) + [jnp.where(edge, beside, 0.0)]
            if side == 0:
                row = [jnp.where(s > 0, v, 0.0) for v in row]
            if side == 2:
                row = [jnp.where(s < ns - 1, v, 0.0) for v in row]
            return row

        def beside_of(row):
            next_first, next_out = pltpu.roll(row[0], 127, 1), pltpu.roll(row[tiles], 127, 1)
            last_last, last_out = pltpu.roll(row[tiles - 1], 1, 1), pltpu.roll(row[tiles], 1, 1)
            right = row[1:tiles] + [jnp.where(last, next_out, next_first), jnp.where(last, next_first, next_out)]
            left = [jnp.where(first, last_out, last_last)] + row[0 : tiles - 1] + [jnp.where(first, last_last, last_out)]
            return [a + b for a, b in zip(left, right)]

        def of_row(n, j):
            row = coef[n, j : j + 1]
            return cut(row) + [row[:, quarter:wide]]

        def around(rows_of, j, own):
            return [
                (a + b) + (n + w * v)
                for a, b, n, w, v in zip(rows_of[j - 1], rows_of[j + 1], beside_of(rows_of[j]), own, rows_of[j])]

        def times(a, b):
            return [v * w for v, w in zip(a, b)]

        six = [6.0] * (tiles + 1)
        for start in range(0, block, 8):
            part = slice(start, start + 8)
            field, state, flux, source = {}, {}, {}, {}
            for e in range(ext):
                field[e] = raw(e, part)
                j = e - 1
                if j >= 1:
                    state[j] = times(of_row(0, j), around(field, j, six))
                j = e - 2
                if j >= 2:
                    flux[j] = times(of_row(2, j), around(state, j, of_row(1, j)))
                j = e - 3
                if j >= 3:
                    source[j] = times(of_row(0, j), around(flux, j, of_row(1, j)))
                j = e - 4
                if j >= 4:
                    again = cut(main[j, held, :].astype(F32)[part])
                    value = [v + 0.1 * w for v, w in zip(again, around(source, j, six))]
                    values[j - HALO, part, :] = jnp.concatenate(value, axis=1)
        for r in range(rows):
            high, low = split(values[r])
            both[r, here, :] = high
            both[r, pl.ds(pl.multiple_of(dirs + base, block), block), :] = low

    before = {b: [] for b in range(len(blocks))}

    def await_own():
        await_bytes(main.at[pl.ds(0, 2 * HALO), pl.ds(0, halves * block), :], own_recv.at[0])
        await_bytes(halos.at[pl.ds(0, 2)], pack_recv.at[1])

    for i, round_stages in enumerate(rounds):
        for p in range(parts):
            for n in round_stages:
                before[i * parts + p].append(functools.partial(forward, n, p))
    before[0].append(await_own)
    for n, stage in enumerate(stages):
        for p in range(parts):
            before[stage[0]].append(functools.partial(await_rows, n, p))

    def step(b, carry):
        for at, actions in before.items():
            if actions:
                @pl.when(b == at)
                def _():
                    for action in actions:
                        action()
        stencil(b)
        return carry

    lax.fori_loop(0, len(blocks), step, 0)

    total = nt_dot(both[0], both[0])
    for r in range(1, rows):
        total = total + nt_dot(both[r], both[r])
    gram[...] = total
    mixed = gram[0:dirs, dirs : 2 * dirs] + gram[dirs : 2 * dirs, 0:dirs]
    local = (gram[0:dirs, 0:dirs] + gram[dirs : 2 * dirs, dirs : 2 * dirs] + mixed) * (1.0 / total_cells)
    result[...] = local.reshape(na, tile, dirs)

    for offset in off_a:
        i, peer = at_a(offset)
        send(result.at[i], part.at[ia], 6, g_recv.at[0], peer)
    part[ia] = result[ia]

    deal[...] = (lax.rem(line, 128) * tiles + line // 128 == spot).astype(F32).astype(BF16)

    def undeal(r, carry):
        both[r] = nn_dot(both[r], deal[...]).astype(BF16)
        return carry

    lax.fori_loop(0, rows, undeal, 0)
    await_bytes(part.at[pl.ds(0, na - 1)], g_recv.at[0])
    part_b[ib] = jnp.sum(part[...], axis=0)
    for offset in off_b:
        send(part_b.at[ib], part_b.at[ib], 7, g_recv.at[1], at_b(offset))
    await_bytes(part_b.at[pl.ds(0, nb - 1)], g_recv.at[1])
    part_c[ia] = jnp.sum(part_b[...], axis=0)
    for offset in off_a:
        send(part_c.at[ia], part_c.at[ia], 8, g_recv.at[2], at_a(offset)[1])
    await_bytes(part_c.at[pl.ds(0, na - 1)], g_recv.at[2])

    whole = part_c[...].reshape(dirs, dirs)
    upper, inverse = factor_and_inverse([whole[t : t + 8] for t in range(0, dirs, 8)])
    factor_ref[...] = upper
    inverse_high, inverse_low = split(inverse)
    inverse_twice = jnp.concatenate([inverse_high, inverse_high], axis=1)

    step_rows = 2
    turned_out = main.at[pl.ds(0, rows)]
    await_bytes(main.at[:, pl.ds(0, (nd - 1) * block), :], sends.at[5])

    def basis_step(j, carry):
        for t in range(step_rows):
            r = j * step_rows + t
            value = nn_dot(inverse_twice, both[r]) + nn_dot(inverse_low, both[r, 0:dirs, :])
            turned_out[r] = value.astype(BF16)
        for k in list(range(2, nd)) + [1]:
            q = lax.rem(d + k, nd)
            here = pl.ds(j * step_rows, step_rows)
            send(turned_out.at[here, dirs_at(q), :], out_ref.at[here, :, cols_at(d)], 9, o_recv.at[0], {"space": s, "dir": q})
        return carry

    lax.fori_loop(0, rows // step_rows, basis_step, 0)
    own_out = pltpu.make_async_copy(turned_out.at[:, dirs_at(d), :], out_ref.at[:, :, cols_at(d)], own_sem.at[1])
    own_out.start()
    await_bytes(halos.at[1, pl.ds(0, nd - 1)], sends.at[0])
    await_bytes(coef_in, sends.at[1])
    await_bytes(main.at[pl.ds(0, 2 * HALO), pl.ds(0, halves * block), :], sends.at[2])
    await_bytes(turned.at[:, :, pl.ds(0, (nd - 1) * quarter)], sends.at[3])
    await_bytes(halos.at[pl.ds(0, 2)], sends.at[4])
    await_bytes(part.at[pl.ds(0, na - 1)], sends.at[6])
    await_bytes(part_b.at[pl.ds(0, nb - 1)], sends.at[7])
    await_bytes(part_c.at[pl.ds(0, na - 1)], sends.at[8])
    own_out.wait()
    away = pl.ds(0, (nd - 1) * quarter)
    await_bytes(out_ref.at[:, :, away], o_recv.at[0])
    await_bytes(out_ref.at[:, :, away], sends.at[9])


def order_kernel(in_ref, factor_in, out_hbm, factor_out, ordered, out_sem, factor_sem):
    count = out_sem.shape[0]
    chunk = in_ref.shape[2] // count
    factor_copy = pltpu.make_async_copy(factor_in, factor_out, factor_sem.at[0])
    factor_copy.start()
    out = []
    for i in range(count):
        here = slice(i * chunk, (i + 1) * chunk)
        ordered[:, :, here] = jnp.swapaxes(in_ref[:, :, here].astype(F32), 0, 1).astype(BF16)
        there = pl.ds(i * chunk, chunk)
        out.append(pltpu.make_async_copy(ordered.at[:, :, there], out_hbm.at[:, :, there], out_sem.at[i]))
        out[i].start()
    for i in range(count):
        out[i].wait()
    factor_copy.wait()


def per_device(ns, nd, directions, depth_coef, sensitivity, obs_weight):
    group, rows, cols = directions.shape
    dirs = group * nd
    nx = 4 if ns >= 8 else ns // 2
    nz = ns // (2 * nx)
    na, nb = nx * nd, nz * 2
    tile = dirs // na
    quarter = cols // nd
    wide = quarter + 128
    ext = rows + 2 * HALO
    cfg = (nd, ns, nx, nz, rows, cols, dirs, rows * ns * cols)
    dma = pltpu.SemaphoreType.DMA
    turned, factor = pl.pallas_call(
        functools.partial(sketch_kernel, cfg),
        out_shape=(jax.ShapeDtypeStruct((rows, group, cols), BF16), jax.ShapeDtypeStruct((dirs, dirs), F32)),
        in_specs=[pl.BlockSpec(memory_space=pltpu.HBM)] * 4,
        out_specs=(pl.BlockSpec(memory_space=pltpu.VMEM),) * 2,
        scratch_shapes=[
            pltpu.VMEM((group, rows, cols), BF16),
            pltpu.VMEM((rows, cols), F32),
            pltpu.VMEM((rows, cols), F32),
            pltpu.VMEM((rows, cols), F32),
            pltpu.VMEM((rows, group, cols), BF16),
            pltpu.VMEM((nd, group, 128), BF16),
            pltpu.VMEM((ext, dirs, quarter), BF16),
            pltpu.VMEM((3, nd, group, 128), BF16),
            pltpu.VMEM((3, ext, wide), F32),
            pltpu.VMEM((3, rows, wide), F32),
            pltpu.VMEM((2, 3, rows, wide), F32),
            pltpu.VMEM((rows, 2 * dirs, quarter), BF16),
            pltpu.VMEM((rows, 16, quarter), F32),
            pltpu.VMEM((quarter, quarter), BF16),
            pltpu.VMEM((2 * dirs, 2 * dirs), F32),
            pltpu.VMEM((na, tile, dirs), F32),
            pltpu.VMEM((nb, tile, dirs), F32),
            pltpu.VMEM((na, tile, dirs), F32),
            pltpu.VMEM((na, tile, dirs), F32),
            dma((10,)), dma((8,)), dma((8,)), dma((2,)), dma((1,)), dma((1,)), dma((3,)), dma((1,)), dma((3,)), dma((4,)),
        ],
        compiler_params=pltpu.CompilerParams(collective_id=0, has_side_effects=True, vmem_limit_bytes=40 * 2**20),
    )(*(pltpu.with_memory_space_constraint(x, pltpu.HBM) for x in (directions, depth_coef, sensitivity, obs_weight)))
    return pl.pallas_call(
        order_kernel,
        out_shape=(jax.ShapeDtypeStruct((group, rows, cols), BF16), jax.ShapeDtypeStruct((dirs, dirs), F32)),
        in_specs=[pl.BlockSpec(memory_space=pltpu.VMEM)] * 2,
        out_specs=(pl.BlockSpec(memory_space=pltpu.HBM),) * 2,
        scratch_shapes=[pltpu.VMEM((group, rows, cols), BF16), dma((4,)), dma((1,))],
        compiler_params=pltpu.CompilerParams(vmem_limit_bytes=40 * 2**20),
    )(turned, factor)


def solution(mesh):
    return jax.shard_map(
        functools.partial(per_device, mesh.shape["space"], mesh.shape["dir"]),
        mesh=mesh,
        in_specs=(P("dir", "space", None), P("space", None), P("space", None), P("space", None)),
        out_specs=(P("dir", "space", None), P()),
        check_vma=False,
    )
```
